32 devices in a mesh: pipe: 4 (over y, x), dp: 8 (over z, core).
Axes of the slice: x: 2, y: 2, z: 4, core: 2. Of those that a mesh axis runs over, the one named last changes fastest.
Arguments:
- video: bfloat16 [4, 8, 3, 16, 8, 128], P(None, 'dp'), may hold values from -6 to 6
- cotangent: bfloat16 [4, 8, 3, 16, 8, 128], P(None, 'dp'), may hold values from -6 to 6
- weights: bfloat16 [4, 3456, 128], P('pipe'), may hold values from -0.109375 to 0.109375
- gains: float32 [4, 128], P('pipe'), may hold values from 0.1 to 1.9
Outputs:
- segment_out: bfloat16 [4, 4, 8, 3, 16, 8, 128], P('pipe', None, 'dp')
- in_grad: bfloat16 [4, 4, 8, 3, 16, 8, 128], P('pipe', None, 'dp')
- weight_grad: float32 [4, 442368], P('pipe', 'dp')
The draws below stay inside these ranges and needn't reach their ends.
All inputs are finite; a program needn't handle non-finite values.
Results may differ from the reference program's by a relative error of at most 0.025.
Values may be sent and summed in bfloat16 or wider, within the bound.
No kernel may reach another device: no remote copies, remote signals or barrier semaphores. Data moves between devices by JAX's collectives and lax.ppermute only.
A program may use at most 64 MiB of HBM per device.

```python
import math
import jax
import jax.numpy as jnp
from jax import lax

C = 128
GROUPS = 32
MB = 4
FRAMES = 3
ROWS = 16
COLS = 8
SEGMENTS = 4
CLIPS = 8


def level_of(own_key, dims, shards, least, high):
    factor_of = 1.0
    for axis_at, parts in shards:
        steps = jax.random.uniform(jax.random.fold_in(jax.random.fold_in(own_key, 6), axis_at), (parts,), jnp.float32, least / len(shards), high / len(shards))
        factor_of = factor_of * jnp.repeat(jnp.exp(steps), dims[axis_at] // parts).reshape((-1,) + (1,) * (len(dims) - 1 - axis_at))
    return factor_of


def scatter_about(own_key, shape, scale, reach, cuts=(), dtype=jnp.bfloat16):
    level = level_of(own_key, shape, cuts, -0.22, 0.18) if cuts else 1.0
    array = jax.random.normal(own_key, shape, jnp.float32) * scale * level
    return jnp.minimum(jnp.maximum(array, -reach), reach).astype(dtype)


def setup_inputs(seed: int = 0) -> dict:
    seeds = jax.random.split(jax.random.key(seed), 5)
    return {
        "video": scatter_about(seeds[0], (MB, CLIPS, FRAMES, ROWS, COLS, C), 1.0, 6.0, ((1, 8),)),
        "cotangent": scatter_about(seeds[1], (MB, CLIPS, FRAMES, ROWS, COLS, C), 1.0, 6.0, ((1, 8),)),
        "weights": scatter_about(seeds[2], (SEGMENTS, 27 * C, C), (27 * C) ** -0.5, 0.109375, ((0, 4),)),
        "gains": jnp.clip(1.0 + 0.18 * jax.random.normal(seeds[3], (SEGMENTS, C), jnp.float32), 0.1, 1.9),
    }


def norm_act(values, gain):
    batch, frames, rows, cols, chans = values.shape
    grouped = values.reshape(batch, frames, rows, cols, GROUPS, chans // GROUPS)
    mean = lax.optimization_barrier(jnp.mean(grouped, axis=(1, 2, 3, 5), keepdims=True))
    centred = grouped - mean
    var = lax.optimization_barrier(jnp.mean(centred * centred, axis=(1, 2, 3, 5), keepdims=True))
    normed = (centred * lax.rsqrt(var + 1e-06)).reshape(values.shape) * gain
    return jax.nn.silu(normed)

def patches(act):
    frames, rows, cols = (act.shape[1], act.shape[2], act.shape[3])
    leading = act[:, :1]
    padded = jnp.concatenate([leading, leading, act], axis=1)
    padded = jnp.pad(padded, ((0, 0), (0, 0), (1, 1), (1, 1), (0, 0)))
    pieces = [padded[:, frame_off:frame_off + frames, row_off:row_off + rows, col_off:col_off + cols, :] for frame_off in range(3) for row_off in range(3) for col_off in range(3)]
    return jnp.concatenate(pieces, axis=-1).reshape(-1, 27 * act.shape[-1])

def forward(inputs, weight, gain):
    values = inputs.astype(jnp.float32)
    act = norm_act(values, gain).astype(jnp.bfloat16)
    cols_mat = patches(act)
    branch = jnp.dot(cols_mat, weight, preferred_element_type=jnp.float32).reshape(inputs.shape)
    return ((values + branch).astype(jnp.bfloat16), cols_mat)

def backward(inputs, grad, weight, gain, cols_mat):
    values = inputs.astype(jnp.float32)
    flat_grad = grad.reshape(-1, grad.shape[-1])
    term = lax.dot_general(cols_mat, flat_grad, (((0,), (0,)), ((), ())), preferred_element_type=jnp.float32)
    grad_cols = lax.dot_general(flat_grad, weight, (((1,), (1,)), ((), ())), preferred_element_type=jnp.float32)
    _, pull_cols = jax.vjp(patches, jnp.zeros(inputs.shape, jnp.float32))
    grad_act = pull_cols(grad_cols)[0]
    _, pull_norm = jax.vjp(lambda field: norm_act(field, gain), values)
    grad_in = grad.astype(jnp.float32) + pull_norm(grad_act)[0]
    return (grad_in.astype(jnp.bfloat16), term)

def reference(video, cotangent, weights, gains):
    inputs_all = []
    outputs_all = []
    current = video
    for segment in range(SEGMENTS):
        inputs_all.append(current)
        current = jnp.stack([forward(current[micro], weights[segment], gains[segment])[0] for micro in range(MB)])
        outputs_all.append(current)
    grad = cotangent
    in_grads = [None] * SEGMENTS
    weight_grads = [None] * SEGMENTS
    scale = 1.0 / math.sqrt(MB * CLIPS * FRAMES * ROWS * COLS)
    for segment in reversed(range(SEGMENTS)):
        total = jnp.zeros((27 * C, C), jnp.float32)
        pieces = []
        for micro in range(MB):
            unit_in = inputs_all[segment][micro]
            cols_mat = forward(unit_in, weights[segment], gains[segment])[1]
            grad_in, term = backward(unit_in, grad[micro], weights[segment], gains[segment], cols_mat)
            total = total + term
            pieces.append(grad_in)
        grad = jnp.stack(pieces)
        in_grads[segment] = grad
        weight_grads[segment] = (total * scale).reshape(-1)
    return (jnp.stack(outputs_all), jnp.stack(in_grads), jnp.stack(weight_grads))
```

```python
import functools
import math

import jax
import jax.numpy as jnp
from jax import lax
from jax.experimental import pallas as pl
from jax.experimental.pallas import tpu as pltpu
from jax.sharding import PartitionSpec as P

GROUPS = 32
EPS = 1e-06
BF, F32 = jnp.bfloat16, jnp.float32
VMEM_LIMIT = 28 * 1024 * 1024
VM = pl.BlockSpec(memory_space=pltpu.VMEM)
SM = pl.BlockSpec(memory_space=pltpu.SMEM)
ANY = pl.BlockSpec(memory_space=pl.ANY)


def call(kernel, out_shape, in_specs, out_specs, scratch=(), flops=0, moved=0):
    return pl.pallas_call(
        kernel,
        out_shape=out_shape,
        in_specs=in_specs,
        out_specs=out_specs,
        scratch_shapes=list(scratch),
        compiler_params=pltpu.CompilerParams(vmem_limit_bytes=VMEM_LIMIT),
        cost_estimate=pl.CostEstimate(flops=flops, bytes_accessed=moved, transcendentals=0),
    )


def swap(value, axis, bits):
    count = lax.axis_size(axis)
    return lax.ppermute(value, axis, [(i, i ^ bits) for i in range(count)])


def group_sum(row, width):
    chans = row.shape[-1]
    lane = lax.broadcasted_iota(jnp.int32, row.shape, 1)
    step = 1
    while step < width:
        up = pltpu.roll(row, chans - step, 1)
        down = pltpu.roll(row, step, 1)
        row = row + jnp.where((lane & step) == 0, up, down)
        step *= 2
    return row


def total_rows(values):
    part = jnp.sum(values.reshape(-1, 8, values.shape[-1]), axis=0)
    return jnp.broadcast_to(jnp.sum(part, axis=0, keepdims=True), part.shape)


def side(frame, cols, step):
    count = frame.shape[0]
    moved = pltpu.roll(frame, (-step) % count, 0)
    col = lax.broadcasted_iota(jnp.int32, frame.shape, 0) & (cols - 1)
    keep = col < cols - 1 if step > 0 else col > 0
    return jnp.where(keep, moved, 0.0)


def row_shift(frame, cols, step):
    gap = jnp.zeros((cols, frame.shape[1]), frame.dtype)
    if step > 0:
        return jnp.concatenate([frame[cols:], gap], axis=0)
    return jnp.concatenate([gap, frame[:-cols]], axis=0)


def three_rows(ref, index, frame, cols, steps):
    chans = frame.shape[1]
    for at, step in enumerate(steps):
        piece = frame if step == 0 else row_shift(frame, cols, step)
        ref[index, :, at * chans : (at + 1) * chans] = piece.astype(BF)


def join_cols(parts, cols, chans, steps):
    total = None
    for at, step in enumerate(steps):
        piece = parts[:, at * chans : (at + 1) * chans]
        piece = piece if step == 0 else side(piece, cols, step)
        total = piece if total is None else total + piece
    return total


def load_weights(sections, place, own, chunks, halves, quarter, buffer, sems, split, only=None):
    chans = own.shape[-1]

    def put(source, rows, slot, index):
        for tap in range(3):
            lanes = pl.ds(tap * chans, chans)
            if split == "c":
                src = source.at[:, tap]
                dst = buffer.at[slot, :, rows, lanes]
            else:
                src = source.at[:, tap]
                dst = buffer.at[slot, :, :, rows, lanes]
            pltpu.make_async_copy(src, dst, sems.at[index]).start()

    def view(ref):
        rows = ref.shape[-2]
        if split == "c":
            return ref.reshape(9, 3, rows, chans)
        return ref.reshape(3, 3, 3, rows, chans)

    def section(k):
        slot = 0 if only is not None else place ^ k
        index = 0 if only is not None else place ^ k
        if k == 0:
            put(view(own), pl.ds(0, chans), slot, index)
            return
        for ref, at in zip(chunks[k - 1], halves):
            rows = pl.multiple_of(at * quarter, quarter)
            put(view(ref), pl.ds(rows, quarter), slot, index)

    for k in range(sections):
        if only is None:
            section(k)
        else:
            pl.when((place ^ k) == only)(functools.partial(section, k))


def wait_weights(buffer, sems, slot):
    pltpu.make_async_copy(buffer.at[slot], buffer.at[slot], sems.at[slot]).wait()


def norm_parts(x32, mean, rstd, gain):
    normed = (x32 - mean) * rstd
    scaled = normed * gain
    return normed, scaled, 1.0 / (1.0 + jnp.exp(-scaled))


def full(row, count):
    return jnp.broadcast_to(row[:1], (count, row.shape[1]))


def forward_kernel(sections, dims, quarter, n_chunk, ids, x_ref, gains, own, *refs):
    frames, rows, cols, chans = dims
    plane, points = rows * cols, frames * rows * cols
    n_in = (sections - 1) * n_chunk
    chunks = [refs[i * n_chunk : (i + 1) * n_chunk] for i in range(sections - 1)]
    outs, stats = refs[n_in : n_in + 2]
    sends = refs[n_in + 2 : n_in + 2 + sections]
    weights, spread, taps, sems = refs[n_in + 2 + sections :]
    place = ids[0]
    load_weights(sections, place, own, chunks, piece_ids(ids, n_chunk), quarter, weights, sems, "c")
    width = chans // GROUPS
    count = float(points * width)
    x32 = x_ref[...].astype(F32)
    for unit in range(sections):
        mean = group_sum(total_rows(x32), width) / count
        cent = x32 - full(mean, points)
        var = group_sum(total_rows(cent * cent), width) / count
        rstd = lax.rsqrt(var + EPS)
        stats[unit, 0:8] = mean
        stats[unit, 8:16] = rstd
        _, scaled, gate = norm_parts(x32, full(mean, points), full(rstd, points), full(gains[unit : unit + 1], points))
        act = scaled * gate
        for k in range(sections):
            @pl.when((place ^ k) == unit)
            def _(k=k):
                sends[k][...] = act.astype(BF)
        for f in range(frames):
            three_rows(spread, f, act[f * plane : (f + 1) * plane], cols, (-1, 0, 1))
        wait_weights(weights, sems, unit)
        spots = [0]
        for a in range(3):
            used = max(1, frames - 2 + a)
            lhs = spread[0:used].reshape(used * plane, 3 * chans)
            rhs = weights[unit, 3 * a : 3 * a + 3].reshape(3 * chans, 3 * chans)
            product = jnp.dot(lhs, rhs, preferred_element_type=F32)
            taps[spots[a] : spots[a] + used] = product.reshape(used, plane, 3 * chans)
            spots.append(spots[a] + used)
        fresh = []
        for f in range(frames):
            total = functools.reduce(lambda u, v: u + v, [taps[spots[a] + max(f - 2 + a, 0)] for a in range(3)])
            fresh.append(x32[f * plane : (f + 1) * plane] + join_cols(total, cols, chans, (-1, 0, 1)))
        for f in range(frames):
            outs[unit, f * plane : (f + 1) * plane] = fresh[f].astype(BF)
        x32 = outs[unit].astype(F32)


def piece_ids(ids, n_chunk):
    per = n_chunk // 2
    return [ids[1] * per + j for j in range(per)] + [(1 - ids[1]) * per + j for j in range(per)]


def unit_backward(dims, x32, grad, stat, gain, weights, slot, spread, taps):
    frames, rows, cols, chans = dims
    plane, points = rows * cols, frames * rows * cols
    width = chans // GROUPS
    count = float(points * width)
    g32 = grad.astype(F32)
    per = [g32[f * plane : (f + 1) * plane] for f in range(frames)]
    contribs = []
    at = 0
    for a in range(3):
        folded = [f for f in range(frames) if f - 2 + a <= 0]
        rest = [f for f in range(frames) if f - 2 + a > 0]
        first = functools.reduce(lambda u, v: u + v, [per[f] for f in folded])
        group = [first] + [per[f] for f in rest]
        for i, piece in enumerate(group):
            three_rows(spread, at + i, piece, cols, (1, 0, -1))
        contribs.append((at, len(group)))
        at += len(group)
    for a in range(3):
        start, used = contribs[a]
        lhs = spread[start : start + used].reshape(used * plane, 3 * chans)
        rhs = weights[slot, a].reshape(3 * chans, 3 * chans)
        product = lax.dot_general(lhs, rhs, (((1,), (1,)), ((), ())), preferred_element_type=F32)
        taps[start : start + used] = product.reshape(used, plane, 3 * chans)
    gact = []
    for f in range(frames):
        total = functools.reduce(lambda u, v: u + v, [taps[start + f] for start, used in contribs if f < used])
        gact.append(join_cols(total, cols, chans, (1, 0, -1)))
    gact = jnp.concatenate(gact, axis=0)
    rstd = full(stat[8:16], points)
    wide_gain = full(gain, points)
    normed, scaled, gate = norm_parts(x32, full(stat[0:8], points), rstd, wide_gain)
    d_normed = gact * (gate * (1.0 + scaled * (1.0 - gate))) * wide_gain
    m1 = group_sum(total_rows(d_normed), width) / count
    m2 = group_sum(total_rows(d_normed * normed), width) / count
    dx = rstd * (d_normed - full(m1, points) - normed * full(m2, points))
    return (g32 + dx).astype(BF)


def backward_kernel(sections, dims, quarter, n_chunk, ids, outs, grad_ref, stats, gains, own, *refs):
    n_in = (sections - 1) * n_chunk
    chunks = [refs[i * n_chunk : (i + 1) * n_chunk] for i in range(sections - 1)]
    grads = refs[n_in]
    sends = refs[n_in + 1 : n_in + 1 + sections]
    weights, spread, taps, sems = refs[n_in + 1 + sections :]
    place = ids[0]
    load_weights(sections, place, own, chunks, piece_ids(ids, n_chunk), quarter, weights, sems, "b")
    grad = grad_ref[...]
    for unit in range(sections - 1, 0, -1):
        wait_weights(weights, sems, unit)
        grad = unit_backward(
            dims, outs[unit - 1].astype(F32), grad, stats[unit], gains[unit : unit + 1], weights, unit, spread, taps
        )
        grads[unit - 1] = grad
        for k in range(sections):
            home = place ^ k
            hit = (home == unit - 1) | (home == unit) if unit == sections - 1 else home == unit - 1
            @pl.when(hit)
            def _(k=k, grad=grad):
                sends[k][...] = grad
    wait_weights(weights, sems, 0)


def first_unit_kernel(sections, dims, quarter, n_chunk, ids, x_ref, outs, grads, stats, gains, own, *refs):
    n_in = (sections - 1) * n_chunk
    chunks = [refs[i * n_chunk : (i + 1) * n_chunk] for i in range(sections - 1)]
    sends = refs[n_in : n_in + sections]
    weights, spread, taps, sems = refs[n_in + sections :]
    place = ids[0]
    load_weights(sections, place, own, chunks, piece_ids(ids, n_chunk), quarter, weights, sems, "b", only=0)
    for k in range(sections):
        home = place ^ k
        sends[k][0] = outs[home]
        sends[k][1] = grads[jnp.maximum(home - 1, 0)]
    wait_weights(weights, sems, 0)
    grad = unit_backward(dims, x_ref[...].astype(F32), grads[0], stats[0], gains[0:1], weights, 0, spread, taps)
    for k in range(sections):
        @pl.when((place ^ k) == 0)
        def _(k=k):
            sends[k][1] = grad


def turn_kernel(dims, n, *refs):
    frames, rows, cols, chans = dims
    plane = rows * cols
    acts, turned = refs[:n], refs[n]
    for k in range(n):
        for f in range(frames):
            frame = acts[k][f * plane : (f + 1) * plane].astype(F32)
            for at, step in enumerate((-1, 0, 1)):
                piece = frame if step == 0 else row_shift(frame, cols, step)
                turned[at * chans : (at + 1) * chans, pl.ds((f * n + k) * plane, plane)] = piece.T.astype(BF)


def term_kernel(sections, dims, n, shares, ids, turned, cot, *refs):
    frames, rows, cols, chans = dims
    plane = rows * cols
    grads = refs[:n]
    rest = refs[n:]
    term = rest[-1] if shares else rest[0]
    right = rest[-2] if shares else rest[1]
    place = ids[0]
    is_last = place == sections - 1
    spots = [0]
    for a in range(3):
        spots.append(spots[-1] + max(1, min(frames, frames - 2 + a)))
    for k in range(n):
        mine = jnp.where(is_last, cot[(place ^ k) % n].astype(F32), grads[k][...].astype(F32))
        per = [mine[f * plane : (f + 1) * plane] for f in range(frames)]
        sides = [[side(p, cols, 1), p, side(p, cols, -1)] for p in per]
        for a in range(3):
            folded = [f for f in range(frames) if f - 2 + a <= 0]
            groups = [folded] + [[f] for f in range(frames) if f - 2 + a > 0]
            for i, group in enumerate(groups):
                for c in range(3):
                    piece = functools.reduce(lambda u, v: u + v, [sides[f][c] for f in group])
                    right[pl.ds(((spots[a] + i) * n + k) * plane, plane), c * chans : (c + 1) * chans] = piece.astype(BF)
    for a in range(3):
        used = (spots[a + 1] - spots[a]) * n * plane
        lhs = turned[:, 0:used]
        rhs = right[pl.ds(spots[a] * n * plane, used), :]
        out = jnp.dot(lhs, rhs, preferred_element_type=F32)
        for b in range(3):
            for c in range(3):
                block = out[b * chans : (b + 1) * chans, c * chans : (c + 1) * chans]
                term[pl.ds(((a * 3 + b) * 3 + c) * chans, chans), :] = block.astype(BF)
    if shares:
        keep, send = rest[0], rest[1]
        core = ids[1]
        size = keep.shape[1]
        for j in range(shares // 2):
            here = pl.multiple_of((2 * j + core) * size, size)
            there = pl.multiple_of((2 * j + 1 - core) * size, size)
            keep[j] = term[pl.ds(here, size), :]
            send[j] = term[pl.ds(there, size), :]


def pair_kernel(count, ids, keep, got, own, *sends):
    level = ids[2]
    for k in range(count):
        at = level ^ k
        total = keep[at].astype(F32) + got[at].astype(F32)
        if k == 0:
            own[...] = total
        else:
            sends[k - 1][...] = total.astype(BF)


def sum_kernel(scale, own, *refs):
    total = own[...]
    for ref in refs[:-1]:
        total = total + ref[...].astype(F32)
    refs[-1][...] = total * scale


def home_kernel(n, ids, *refs):
    pieces, seg, ing = refs[:n], refs[n], refs[n + 1]
    for k in range(n):
        at = (ids[0] ^ k) % n
        seg[at] = pieces[k][0]
        ing[at] = pieces[k][1]


def gather_chunks(weights, core, sections, parts):
    taps, chans = weights.shape[0], weights.shape[-1]
    quarter = weights.shape[1] // (2 * parts)
    cut = weights.reshape(taps, 2 * parts, quarter, chans)
    mine = [lax.dynamic_index_in_dim(cut, core * parts + j, 1, False) for j in range(parts)]
    got = {}
    if sections == 4 and parts == 2:
        first = swap(mine[0], "pipe", 1)
        second = swap(mine[1], "pipe", 2)
        got[1] = [first, swap(mine[1], "pipe", 1)]
        got[2] = [swap(mine[0], "pipe", 2), second]
        got[3] = [swap(first, "pipe", 2), swap(second, "pipe", 1)]
    else:
        for k in range(1, sections):
            got[k] = [swap(piece, "pipe", k) for piece in mine]
    return [got[k] + [swap(piece, "dp", 1) for piece in got[k]] for k in range(1, sections)]


def body(video, cotangent, weights, gains):
    sections = lax.axis_size("pipe")
    ranks = lax.axis_size("dp")
    place = lax.axis_index("pipe")
    rank = lax.axis_index("dp")
    core = rank % 2
    ids = jnp.stack([place, core, rank // 2]).astype(jnp.int32)
    micro, clips, frames, rows, cols, chans = video.shape
    points = frames * rows * cols
    dims = (frames, rows, cols, chans)
    parts = 2
    n_chunk = 2 * parts
    quarter = chans // n_chunk

    video = video.reshape(micro, points, chans)
    cot = cotangent.reshape(micro, points, chans)
    kernel_rows = weights.reshape(27, chans, chans)
    chunks = gather_chunks(kernel_rows, core, sections, parts)
    flat = [piece for group in chunks for piece in group]
    all_gains = lax.all_gather(gains[0], "pipe")
    mb = place % micro
    x = lax.dynamic_index_in_dim(video, mb, 0, False)
    grad = lax.dynamic_index_in_dim(cot, mb, 0, False)

    act_shape = jax.ShapeDtypeStruct((points, chans), BF)
    two = jax.ShapeDtypeStruct((2, points, chans), BF)
    unit_flops = 2 * points * 27 * chans * chans
    spread = pltpu.VMEM((2 * frames, rows * cols, 3 * chans), BF)
    taps = pltpu.VMEM((2 * frames, rows * cols, 3 * chans), F32)
    sems = pltpu.SemaphoreType.DMA((sections,))

    outs, stats, *acts = call(
        functools.partial(forward_kernel, sections, dims, quarter, n_chunk),
        [jax.ShapeDtypeStruct((sections, points, chans), BF), jax.ShapeDtypeStruct((sections, 16, chans), F32)]
        + [act_shape] * sections,
        [SM, VM, VM, ANY] + [ANY] * len(flat),
        [VM] * (2 + sections),
        [pltpu.VMEM((sections, 9, chans, 3 * chans), BF), spread, taps, sems],
        flops=4 * sections * unit_flops,
    )(ids, x, all_gains, kernel_rows, *flat)

    n = min(sections, micro)
    acts_home = [acts[0]] + [swap(acts[k], "pipe", k) for k in range(1, n)]

    grads, *gsends = call(
        functools.partial(backward_kernel, sections, dims, quarter, n_chunk),
        [jax.ShapeDtypeStruct((sections - 1, points, chans), BF)] + [act_shape] * sections,
        [SM, VM, VM, VM, VM, ANY] + [ANY] * len(flat),
        [VM] * (1 + sections),
        [pltpu.VMEM((sections, 3, 3, chans, 3 * chans), BF), spread, taps, sems],
        flops=4 * (sections - 1) * unit_flops,
    )(ids, outs, grad, stats, all_gains, kernel_rows, *flat)
    grads_home = [gsends[0]] + [swap(gsends[k], "pipe", k) for k in range(1, n)]

    osends = call(
        functools.partial(first_unit_kernel, sections, dims, quarter, n_chunk),
        [two] * sections,
        [SM, VM, VM, VM, VM, VM, ANY] + [ANY] * len(flat),
        [VM] * sections,
        [pltpu.VMEM((1, 3, 3, chans, 3 * chans), BF), spread, taps, pltpu.SemaphoreType.DMA((1,))],
        flops=4 * unit_flops,
    )(ids, x, outs, grads, stats, all_gains, kernel_rows, *flat)

    turned = call(
        functools.partial(turn_kernel, dims, n),
        jax.ShapeDtypeStruct((3 * chans, n * points), BF),
        [VM] * n,
        VM,
        flops=unit_flops,
    )(*acts_home)

    size = 27 * chans // ranks
    spots = sum(max(1, min(frames, frames - 2 + a)) for a in range(3))
    right = pltpu.VMEM((spots * n * rows * cols, 3 * chans), BF)
    half = jax.ShapeDtypeStruct((ranks // 2, size, chans), BF)
    levels = ranks // 2
    if size % 16 == 0:
        keep, send = call(
            functools.partial(term_kernel, sections, dims, n, ranks),
            [half, half],
            [SM, VM, VM] + [VM] * n,
            [VM, VM],
            [right, pltpu.VMEM((27 * chans, chans), BF)],
            flops=n * unit_flops,
        )(ids, turned, cot, *grads_home)
    else:
        term = call(
            functools.partial(term_kernel, sections, dims, n, 0),
            jax.ShapeDtypeStruct((27 * chans, chans), BF),
            [SM, VM, VM] + [VM] * n,
            VM,
            [right],
            flops=n * unit_flops,
        )(ids, turned, cot, *grads_home)
        shares = term.reshape(levels, 2, size, chans)
        keep = lax.dynamic_index_in_dim(shares, core, 1, False)
        send = lax.dynamic_index_in_dim(shares, 1 - core, 1, False)
    got = swap(send, "dp", 1)
    piece = jax.ShapeDtypeStruct((size, chans), BF)
    own, *zsends = call(
        functools.partial(pair_kernel, levels),
        [jax.ShapeDtypeStruct((size, chans), F32)] + [piece] * (levels - 1),
        [SM, VM, VM],
        [VM] * levels,
    )(ids, keep, got)
    arrived = [swap(zsends[k - 1], "dp", 2 * k) for k in range(1, levels)]

    scale = 1.0 / math.sqrt(micro * clips * ranks * points)
    share = call(
        functools.partial(sum_kernel, scale),
        jax.ShapeDtypeStruct((size, chans), F32),
        [VM] * levels,
        VM,
    )(own, *arrived)

    homes = [osends[0]] + [swap(osends[k], "pipe", k) for k in range(1, n)]
    seg, ing = call(
        functools.partial(home_kernel, n),
        [jax.ShapeDtypeStruct((micro, points, chans), BF)] * 2,
        [SM] + [VM] * n,
        [VM, VM],
    )(ids, *homes)
    shape = (1, micro, clips, frames, rows, cols, chans)
    return (seg.reshape(shape), ing.reshape(shape), share.reshape(1, size * chans))


def solution(mesh):
    in_specs = (
        P(None, "dp", None, None, None, None),
        P(None, "dp", None, None, None, None),
        P("pipe", None, None),
        P("pipe", None),
    )
    out_specs = (
        P("pipe", None, "dp", None, None, None, None),
        P("pipe", None, "dp", None, None, None, None),
        P("pipe", "dp"),
    )
    return jax.shard_map(body, mesh=mesh, in_specs=in_specs, out_specs=out_specs, check_vma=False)
```

```python
import functools
import math

import jax
import jax.numpy as jnp
from jax import lax
from jax.experimental import pallas as pl
from jax.experimental.pallas import tpu as pltpu
from jax.sharding import PartitionSpec as P

GROUPS = 32
EPS = 1e-06
BF, F32 = jnp.bfloat16, jnp.float32
VMEM_LIMIT = 28 * 1024 * 1024
VM = pl.BlockSpec(memory_space=pltpu.VMEM)
SM = pl.BlockSpec(memory_space=pltpu.SMEM)
ANY = pl.BlockSpec(memory_space=pl.ANY)
HBM = pl.BlockSpec(memory_space=pltpu.HBM)


def call(kernel, out_shape, in_specs, out_specs, scratch=(), flops=0, moved=0, limit=VMEM_LIMIT):
    return pl.pallas_call(
        kernel,
        out_shape=out_shape,
        in_specs=in_specs,
        out_specs=out_specs,
        scratch_shapes=list(scratch),
        compiler_params=pltpu.CompilerParams(vmem_limit_bytes=limit),
        cost_estimate=pl.CostEstimate(flops=flops, bytes_accessed=moved, transcendentals=0),
    )


def swap(value, axis, bits):
    count = lax.axis_size(axis)
    return lax.ppermute(value, axis, [(i, i ^ bits) for i in range(count)])


def lane_partner(row, step):
    lane = lax.broadcasted_iota(jnp.int32, row.shape, 1)
    ahead = pltpu.roll(row, row.shape[1] - step, 1)
    return jnp.where((lane & step) == 0, ahead, pltpu.roll(row, step, 1))


def tree(parts):
    parts = list(parts)
    while len(parts) > 1:
        pairs = [u + v for u, v in zip(parts[::2], parts[1::2])]
        parts = pairs + parts[len(pairs) * 2 :]
    return parts[0]


def tiles(values):
    return [values[i : i + 8] for i in range(0, values.shape[0], 8)]


def group_sum(values, width):
    row = tree(tiles(values))
    for step in (4, 2, 1):
        row = row + pltpu.roll(row, step, 0)
    step = 1
    while step < width:
        row = row + lane_partner(row, step)
        step *= 2
    return row


def statistics(x32, width):
    parts = tiles(x32)
    pivot = parts[0]
    gaps = [part - pivot for part in parts[1:]]
    first = tree(gaps)
    second = tree([gap * gap for gap in gaps])
    count = float(len(parts))
    mean = pivot + first * (1.0 / count)
    spread = jnp.maximum(second - first * first * (1.0 / count), 0.0)

    def join(mean, spread, other, other_spread):
        gap = mean - other
        return (mean + other) * 0.5, spread + other_spread + gap * gap * (0.5 * count)

    for step in (4, 2, 1):
        mean, spread = join(mean, spread, pltpu.roll(mean, step, 0), pltpu.roll(spread, step, 0))
        count *= 2.0
    step = 1
    while step < width:
        mean, spread = join(mean, spread, lane_partner(mean, step), lane_partner(spread, step))
        count *= 2.0
        step *= 2
    return mean, lax.rsqrt(spread * (1.0 / count) + EPS)


def side(frame, cols, step):
    lines = frame.reshape(-1, cols, frame.shape[1])
    moved = pltpu.roll(lines, (-step) % cols, 1)
    col = lax.broadcasted_iota(jnp.int32, lines.shape, 1)
    keep = col < cols - 1 if step > 0 else col > 0
    return jnp.where(keep, moved, 0.0).reshape(frame.shape)


def row_shift(frame, cols, step):
    gap = jnp.zeros((cols, frame.shape[1]), frame.dtype)
    if step > 0:
        return jnp.concatenate([frame[cols:], gap], axis=0)
    return jnp.concatenate([gap, frame[:-cols]], axis=0)


def three_rows(frame, cols, steps):
    return [(frame if step == 0 else row_shift(frame, cols, step)).astype(BF) for step in steps]


def put_rows(spread, index, a, pieces):
    for b, piece in enumerate(pieces):
        chans = piece.shape[1]
        at = (3 * a + b) * chans
        spread[index, :, at : at + chans] = piece


def join_cols(parts, cols, chans, steps):
    total = None
    for at, step in enumerate(steps):
        piece = parts[:, at * chans : (at + 1) * chans]
        piece = piece if step == 0 else side(piece, cols, step)
        total = piece if total is None else total + piece
    return total


def copies_of(chunks, halves, target, sem):
    quarter = chunks[0].shape[1]
    return [
        pltpu.make_async_copy(
            ref.at[0 : target.shape[0]], target.at[:, pl.ds(pl.multiple_of(at * quarter, quarter), quarter), :], sem
        )
        for ref, at in zip(chunks, halves)
    ]


def piece_ids(ids, n_chunk):
    per = n_chunk // 2
    return [ids[1] * per + j for j in range(per)] + [(1 - ids[1]) * per + j for j in range(per)]


def forward_matrix(taps):
    chans = taps.shape[-1]
    parts = taps.reshape(9, 3, chans, chans)
    return jnp.concatenate([parts[:, c].reshape(9 * chans, chans) for c in range(3)], axis=1)


def backward_matrix(taps):
    chans = taps.shape[-1]
    parts = taps.reshape(9, 3 * chans, chans)
    return jnp.concatenate([parts[ab] for ab in range(9)], axis=1)


def norm_parts(x32, mean, rstd, gain):
    normed = (x32 - mean) * rstd
    scaled = normed * gain
    return normed, scaled, 0.5 * jnp.tanh(0.5 * scaled) + 0.5


def full(row, count):
    return jnp.broadcast_to(row[:1], (count, row.shape[1]))


def spread_forward(dims, values, found, gain, spread):
    frames, rows, cols, chans = dims
    plane, points = rows * cols, frames * rows * cols
    for k, x32 in enumerate(values):
        mean, rstd = found[k]
        _, scaled, gate = norm_parts(x32, full(mean, points), full(rstd, points), full(gain, points))
        act = scaled * gate
        for source in range(frames):
            pieces = three_rows(act[source * plane : (source + 1) * plane], cols, (-1, 0, 1))
            for f in range(frames):
                for a in range(3):
                    if max(f - 2 + a, 0) == source:
                        put_rows(spread, k * frames + f, a, pieces)


def cut_kernel(parts, ids, gain, own, *refs):
    pieces, sems = refs[:parts], refs[parts]
    taps, quarter = own.shape[0], pieces[0].shape[1]
    copies = []
    for j in range(parts):
        rows = pl.ds(pl.multiple_of((ids[1] * parts + j) * quarter, quarter), quarter)
        copies.append(pltpu.make_async_copy(own.at[:, rows, :], pieces[j].at[0:taps], sems.at[j]))
    for copy in copies:
        copy.start()
    wide = full(gain[...], quarter)
    high = wide.astype(BF).astype(F32)
    middle = (wide - high).astype(BF).astype(F32)
    low = wide - high - middle
    row = lax.broadcasted_iota(jnp.int32, wide.shape, 0)
    pieces[0][taps] = jnp.where(row == 0, high, jnp.where(row == 1, middle, low)).astype(BF)
    for copy in copies:
        copy.wait()


def forward_kernel(sections, dims, ids, x_ref, gain, *refs):
    frames, rows, cols, chans = dims
    plane = rows * cols
    n_chunk = (len(refs) - 8 - sections) // sections
    chunks = [refs[k * n_chunk : (k + 1) * n_chunk] for k in range(sections)]
    refs = refs[sections * n_chunk :]
    outs, stats, every = refs[:3]
    sends = refs[3 : 3 + sections]
    spread, product, gain_rows, gain_sem, sems = refs[3 + sections :]
    place = ids[0]
    taps = every.shape[1]
    copies = [
        pltpu.make_async_copy(chunks[k][0].at[taps], gain_rows.at[k - 1], gain_sem.at[k - 1])
        for k in range(1, sections)
    ]
    for copy in copies:
        copy.start()

    def start(slot, k):
        for copy in copies_of(chunks[k], piece_ids(ids, n_chunk), every.at[slot], sems.at[slot]):
            copy.start()

    for slot in range(sections):
        for k in range(sections):
            pl.when((place ^ k) == slot)(functools.partial(start, slot, k))
    stats[place, 16:24] = full(gain[...], 8)
    for k in range(1, sections):
        copies[k - 1].wait()
        parts = gain_rows[k - 1].astype(F32)
        stats[place ^ k, 16:24] = full(parts[0:1] + parts[1:2] + parts[2:3], 8)
    x = x_ref[...]
    for unit in range(sections):
        for k in range(sections):
            @pl.when((place ^ k) == unit)
            def _(k=k, x=x):
                sends[k][...] = x

        x32 = x.astype(F32)
        mean, rstd = statistics(x32, chans // GROUPS)
        stats[unit, 0:8], stats[unit, 8:16] = mean, rstd
        spread_forward(dims, [x32], [(mean, rstd)], stats[unit, 16:17], spread)
        pltpu.make_async_copy(every.at[unit], every.at[unit], sems.at[unit]).wait()
        lhs = spread[...].reshape(frames * plane, 9 * chans)
        product[...] = jnp.dot(lhs, forward_matrix(every[unit]), preferred_element_type=F32)
        for f in range(frames):
            spot = slice(f * plane, (f + 1) * plane)
            joined = join_cols(product[spot], cols, chans, (-1, 0, 1))
            outs[unit, spot] = (x32[spot] + joined).astype(BF)
        x = outs[unit]


def turn_kernel(dims, n, gain, *refs):
    frames, rows, cols, chans = dims
    plane, points = rows * cols, frames * rows * cols
    xs, (turned, stats) = refs[:n], refs[n:]
    for k in range(n):
        x32 = xs[k][...].astype(F32)
        mean, rstd = statistics(x32, chans // GROUPS)
        stats[k, 0:8], stats[k, 8:16] = mean, rstd
        _, scaled, gate = norm_parts(x32, full(mean, points), full(rstd, points), full(gain[...], points))
        act = (scaled * gate).astype(BF).astype(F32)
        for f in range(frames):
            frame = act[f * plane : (f + 1) * plane]
            for at, step in enumerate((-1, 0, 1)):
                piece = frame if step == 0 else row_shift(frame, cols, step)
                turned[at * chans : (at + 1) * chans, pl.ds((f * n + k) * plane, plane)] = piece.T.astype(BF)


def home_forward_kernel(dims, n, ids, stats, gain, own, *refs):
    frames, rows, cols, chans = dims
    plane = rows * cols
    xs, (seg, spread) = refs[:n], refs[n:]
    values = [ref[...].astype(F32) for ref in xs]
    known = [(stats[k, 0:8], stats[k, 8:16]) for k in range(n)]
    spread_forward(dims, values, known, gain[...], spread)
    lhs = spread[...].reshape(n * frames * plane, 9 * chans)
    product = jnp.dot(lhs, forward_matrix(own[...]), preferred_element_type=F32)
    for k in range(n):
        at = (ids[0] ^ k) % n
        for f in range(frames):
            spot = slice(f * plane, (f + 1) * plane)
            joined = join_cols(product[(k * frames + f) * plane : (k * frames + f + 1) * plane], cols, chans, (-1, 0, 1))
            seg[at, spot] = (values[k][spot] + joined).astype(BF)


def unit_backward(dims, x32, grad, stat, gain, multiply, spread):
    frames, rows, cols, chans = dims
    plane, points = rows * cols, frames * rows * cols
    width = chans // GROUPS
    count = float(points * width)
    g32 = grad.astype(F32)
    per = [g32[f * plane : (f + 1) * plane] for f in range(frames)]
    for f in range(frames):
        for a in range(3):
            sources = [q for q in range(frames) if max(q - 2 + a, 0) == f]
            if sources:
                total = functools.reduce(lambda u, v: u + v, [per[q] for q in sources])
                put_rows(spread, f, a, three_rows(total, cols, (1, 0, -1)))
            else:
                put_rows(spread, f, a, [jnp.zeros((plane, chans), BF)] * 3)
    product = multiply(spread[...].reshape(points, 9 * chans))
    gact = jnp.concatenate(
        [join_cols(product[f * plane : (f + 1) * plane], cols, chans, (1, 0, -1)) for f in range(frames)], axis=0
    )
    rstd = full(stat[8:16], points)
    wide_gain = full(gain, points)
    normed, scaled, gate = norm_parts(x32, full(stat[0:8], points), rstd, wide_gain)
    d_normed = gact * (gate * (1.0 + scaled * (1.0 - gate))) * wide_gain
    m1 = group_sum(d_normed, width) * (1.0 / count)
    m2 = group_sum(d_normed * normed, width) * (1.0 / count)
    dx = rstd * (d_normed - full(m1, points) - normed * full(m2, points))
    return (g32 + dx).astype(BF)


def times_transposed(lhs, taps):
    return lax.dot_general(lhs, backward_matrix(taps), (((1,), (1,)), ((), ())), preferred_element_type=F32)


def backward_kernel(sections, dims, ids, outs, grad_ref, stats, every, *refs):
    sends, spread = refs[:sections], refs[sections]
    place = ids[0]
    grad = grad_ref[...]
    for k in range(sections):
        @pl.when((place ^ k) == sections - 1)
        def _(k=k, grad=grad):
            sends[k][...] = grad
    for unit in range(sections - 1, 0, -1):

        def multiply(lhs, unit=unit):
            return times_transposed(lhs, every[unit])

        grad = unit_backward(dims, outs[unit - 1].astype(F32), grad, stats[unit], stats[unit, 16:17], multiply, spread)
        for k in range(sections):
            @pl.when((place ^ k) == unit - 1)
            def _(k=k, grad=grad):
                sends[k][...] = grad


def home_backward_kernel(dims, n, first, last, ids, stats, gain, own, *refs):
    count = last - first
    xs, grads = refs[:count], refs[count : 2 * count]
    refs = refs[2 * count :]
    done = refs[:first] if last == n else ()
    outs, spread = refs[len(done) : -1], refs[-1]
    place = ids[0]
    for k in range(len(done)):
        outs[0][(place ^ k) % n] = done[k][...]
    for i in range(count):
        result = unit_backward(
            dims,
            xs[i][...].astype(F32),
            grads[i][...],
            stats[first + i],
            gain[...],
            lambda lhs: times_transposed(lhs, own[...]),
            spread,
        )
        if last == n:
            outs[0][(place ^ (first + i)) % n] = result
        else:
            outs[i][...] = result


def term_kernel(dims, n, shares, ids, turned, *refs):
    frames, rows, cols, chans = dims
    plane = rows * cols
    grads = refs[:n]
    rest = refs[n:]
    term = rest[-1] if shares else rest[0]
    right = rest[-2] if shares else rest[1]
    spots = [0]
    for a in range(3):
        spots.append(spots[-1] + max(1, min(frames, frames - 2 + a)))
    for k in range(n):
        mine = grads[k][...].astype(F32)
        per = [mine[f * plane : (f + 1) * plane] for f in range(frames)]
        sides = [[side(p, cols, 1), p, side(p, cols, -1)] for p in per]
        for a in range(3):
            folded = [f for f in range(frames) if f - 2 + a <= 0]
            groups = [folded] + [[f] for f in range(frames) if f - 2 + a > 0]
            for i, group in enumerate(groups):
                for c in range(3):
                    piece = functools.reduce(lambda u, v: u + v, [sides[f][c] for f in group])
                    right[pl.ds(((spots[a] + i) * n + k) * plane, plane), c * chans : (c + 1) * chans] = piece.astype(BF)
    for a in range(3):
        used = (spots[a + 1] - spots[a]) * n * plane
        lhs = turned[:, 0:used]
        rhs = right[pl.ds(spots[a] * n * plane, used), :]
        out = jnp.dot(lhs, rhs, preferred_element_type=F32)
        for b in range(3):
            for c in range(3):
                block = out[b * chans : (b + 1) * chans, c * chans : (c + 1) * chans]
                term[pl.ds(((a * 3 + b) * 3 + c) * chans, chans), :] = block.astype(BF)
    if shares:
        keep, send = rest[0], rest[1]
        core = ids[1]
        size = keep.shape[1]
        for j in range(shares // 2):
            here = pl.multiple_of((2 * j + core) * size, size)
            there = pl.multiple_of((2 * j + 1 - core) * size, size)
            keep[j] = term[pl.ds(here, size), :]
            send[j] = term[pl.ds(there, size), :]


def pair_kernel(count, ids, keep, got, own, *sends):
    level = ids[2]
    for k in range(count):
        at = level ^ k
        total = keep[at].astype(F32) + got[at].astype(F32)
        if k == 0:
            own[...] = total
        else:
            sends[k - 1][...] = total.astype(BF)


def sum_kernel(scale, own, *refs):
    total = own[...]
    for ref in refs[:-1]:
        total = total + ref[...].astype(F32)
    refs[-1][...] = total * scale


def gather_chunks(mine, sections, ride):
    parts = len(mine)
    got = {}
    if sections == 4 and parts == 2:
        first = swap(mine[0], "pipe", 1)
        second = swap(mine[1], "pipe", 2)
        first, *ride = lax.optimization_barrier((first, *ride))
        got[1] = [first, swap(mine[1], "pipe", 1)]
        got[2] = [swap(mine[0], "pipe", 2), second]
        got[3] = [swap(first, "pipe", 2), swap(second, "pipe", 1)]
    else:
        for k in range(1, sections):
            got[k] = [swap(piece, "pipe", k) for piece in mine]
    return got, ride


def body(video, cotangent, weights, gains):
    sections = lax.axis_size("pipe")
    ranks = lax.axis_size("dp")
    place = lax.axis_index("pipe")
    rank = lax.axis_index("dp")
    core = lax.rem(rank, 2)
    micro, clips, frames, rows, cols, chans = video.shape
    ids = jnp.stack([place, core, lax.div(rank, 2)]).astype(jnp.int32)
    points = frames * rows * cols
    dims = (frames, rows, cols, chans)
    parts = 2
    n_chunk = 2 * parts
    quarter = chans // n_chunk

    video = video.reshape(micro, points, chans)
    cot = cotangent.reshape(micro, points, chans)
    kernel_rows = weights.reshape(27, chans, chans)
    gain_rows = jnp.broadcast_to(gains, (8, chans))
    mine = call(
        functools.partial(cut_kernel, parts),
        [jax.ShapeDtypeStruct((27 + (j == 0), quarter, chans), BF) for j in range(parts)],
        [SM, VM, ANY],
        [VM] * parts,
        [pltpu.SemaphoreType.DMA((parts,))],
    )(ids, gain_rows, kernel_rows)
    x = lax.dynamic_index_in_dim(video, lax.rem(place, micro), 0, False)
    grad = lax.dynamic_index_in_dim(cot, lax.rem(place, micro), 0, False)
    got, (x, grad) = gather_chunks(mine, sections, (x, grad))
    got[0] = list(mine)
    flat = [piece for k in range(sections) for piece in got[k] + [swap(piece, "dp", 1) for piece in got[k]]]

    act_shape = jax.ShapeDtypeStruct((points, chans), BF)
    unit_flops = 2 * points * 27 * chans * chans
    n = min(sections, micro)
    spots = sum(max(1, frames - 2 + a) for a in range(3))

    def spread(count):
        return pltpu.VMEM((count * frames, rows * cols, 9 * chans), BF)

    product = pltpu.VMEM((points, 3 * chans), F32)

    outs, stats, every, *xsends = call(
        functools.partial(forward_kernel, sections, dims),
        [
            jax.ShapeDtypeStruct((sections, points, chans), BF),
            jax.ShapeDtypeStruct((sections, 24, chans), F32),
            jax.ShapeDtypeStruct((sections, 27, chans, chans), BF),
        ]
        + [act_shape] * sections,
        [SM, VM, VM] + [ANY] * len(flat),
        [VM] * (3 + sections),
        [
            spread(1),
            product,
            pltpu.VMEM((sections - 1, quarter, chans), BF),
            pltpu.SemaphoreType.DMA((sections - 1,)),
            pltpu.SemaphoreType.DMA((sections,)),
        ],
        flops=4 * sections * unit_flops,
    )(ids, x, gain_rows, *flat)
    xs_home = [xsends[0]] + [swap(xsends[k], "pipe", k) for k in range(1, n)]

    gsends = call(
        functools.partial(backward_kernel, sections, dims),
        [act_shape] * sections,
        [SM] + [VM] * 4,
        [VM] * sections,
        [spread(1)],
        flops=4 * (sections - 1) * unit_flops,
    )(ids, outs, grad, stats, every)
    grads_home = [gsends[0]] + [swap(gsends[k], "pipe", k) for k in range(1, n)]

    turned, home_stats = call(
        functools.partial(turn_kernel, dims, n),
        [jax.ShapeDtypeStruct((3 * chans, n * points), BF), jax.ShapeDtypeStruct((n, 16, chans), F32)],
        [VM] * (1 + n),
        [VM] * 2,
        flops=n * unit_flops,
    )(gain_rows, *xs_home)

    def home_forward(ids):
        return call(
            functools.partial(home_forward_kernel, dims, n),
            jax.ShapeDtypeStruct((micro, points, chans), BF),
            [SM, VM, VM, VM] + [VM] * n,
            VM,
            [spread(n)],
            flops=4 * n * unit_flops,
        )(ids, home_stats, gain_rows, kernel_rows, *xs_home)

    def home_backward(first, last, done, ids):
        count = last - first
        return call(
            functools.partial(home_backward_kernel, dims, n, first, last),
            [jax.ShapeDtypeStruct((micro, points, chans), BF)] if last == n else [act_shape] * count,
            [SM, VM, VM, VM] + [VM] * (2 * count + len(done)),
            [VM] * (1 if last == n else count),
            [spread(1)],
            flops=4 * count * unit_flops,
        )(ids, home_stats, gain_rows, kernel_rows, *xs_home[first:last], *grads_home[first:last], *done)

    size = 27 * chans // ranks
    right = pltpu.VMEM((spots * n * rows * cols, 3 * chans), BF)
    half = jax.ShapeDtypeStruct((ranks // 2, size, chans), BF)
    levels = ranks // 2
    if size % 16 == 0:
        keep, send = call(
            functools.partial(term_kernel, dims, n, ranks),
            [half, half],
            [SM, VM] + [VM] * n,
            [VM, VM],
            [right, pltpu.VMEM((27 * chans, chans), BF)],
            flops=n * unit_flops,
        )(ids, turned, *grads_home)
    else:
        term = call(
            functools.partial(term_kernel, dims, n, 0),
            jax.ShapeDtypeStruct((27 * chans, chans), BF),
            [SM, VM] + [VM] * n,
            VM,
            [right],
            flops=n * unit_flops,
        )(ids, turned, *grads_home)
        shares = term.reshape(levels, 2, size, chans)
        keep = lax.dynamic_index_in_dim(shares, core, 1, False)
        send = lax.dynamic_index_in_dim(shares, 1 - core, 1, False)
    got = swap(send, "dp", 1)
    early = home_backward(0, n // 2, (), ids)
    piece = jax.ShapeDtypeStruct((size, chans), BF)
    own, *zsends = call(
        functools.partial(pair_kernel, levels),
        [jax.ShapeDtypeStruct((size, chans), F32)] + [piece] * (levels - 1),
        [SM, VM, VM],
        [VM] * levels,
    )(ids, keep, got)
    arrived = [swap(zsends[k - 1], "dp", 2 * k) for k in range(levels - 1, 0, -1)]

    scale = 1.0 / math.sqrt(micro * clips * ranks * points)
    share = call(
        functools.partial(sum_kernel, scale),
        jax.ShapeDtypeStruct((size, chans), F32),
        [VM] * levels,
        VM,
    )(own, *arrived)

    late, _ = lax.optimization_barrier((ids, own))
    (ing,) = home_backward(n // 2, n, early, late)
    seg = home_forward(late)
    shape = (1, micro, clips, frames, rows, cols, chans)
    return (seg.reshape(shape), ing.reshape(shape), share.reshape(1, size * chans))


def solution(mesh):
    in_specs = (
        P(None, "dp", None, None, None, None),
        P(None, "dp", None, None, None, None),
        P("pipe", None, None),
        P("pipe", None),
    )
    out_specs = (
        P("pipe", None, "dp", None, None, None, None),
        P("pipe", None, "dp", None, None, None, None),
        P("pipe", "dp"),
    )
    return jax.shard_map(body, mesh=mesh, in_specs=in_specs, out_specs=out_specs, check_vma=False)
```

```python
import functools
import math

import jax
import jax.numpy as jnp
from jax import lax
from jax.experimental import pallas as pl
from jax.experimental.pallas import tpu as pltpu
from jax.sharding import PartitionSpec as P

GROUPS = 32
EPS = 1e-06
BF, F32 = jnp.bfloat16, jnp.float32
VMEM_LIMIT = 28 * 1024 * 1024
VM = pl.BlockSpec(memory_space=pltpu.VMEM)
SM = pl.BlockSpec(memory_space=pltpu.SMEM)
ANY = pl.BlockSpec(memory_space=pl.ANY)
HBM = pl.BlockSpec(memory_space=pltpu.HBM)


def call(kernel, out_shape, in_specs, out_specs, scratch=(), flops=0, moved=0, limit=VMEM_LIMIT):
    return pl.pallas_call(
        kernel,
        out_shape=out_shape,
        in_specs=in_specs,
        out_specs=out_specs,
        scratch_shapes=list(scratch),
        compiler_params=pltpu.CompilerParams(vmem_limit_bytes=limit),
        cost_estimate=pl.CostEstimate(flops=flops, bytes_accessed=moved, transcendentals=0),
    )


def swap(value, axis, bits):
    count = lax.axis_size(axis)
    return lax.ppermute(value, axis, [(i, i ^ bits) for i in range(count)])


def lane_partner(row, step):
    lane = lax.broadcasted_iota(jnp.int32, row.shape, 1)
    ahead = pltpu.roll(row, row.shape[1] - step, 1)
    return jnp.where((lane & step) == 0, ahead, pltpu.roll(row, step, 1))


def tree(parts):
    parts = list(parts)
    while len(parts) > 1:
        pairs = [u + v for u, v in zip(parts[::2], parts[1::2])]
        parts = pairs + parts[len(pairs) * 2 :]
    return parts[0]


def tiles(values):
    return [values[i : i + 8] for i in range(0, values.shape[0], 8)]


def group_sum(values, width):
    row = tree(tiles(values))
    for step in (4, 2, 1):
        row = row + pltpu.roll(row, step, 0)
    step = 1
    while step < width:
        row = row + lane_partner(row, step)
        step *= 2
    return row


def statistics(x32, width):
    parts = tiles(x32)
    pivot = parts[0]
    gaps = [part - pivot for part in parts[1:]]
    first = tree(gaps)
    second = tree([gap * gap for gap in gaps])
    count = float(len(parts))
    mean = pivot + first * (1.0 / count)
    spread = jnp.maximum(second - first * first * (1.0 / count), 0.0)

    def join(mean, spread, other, other_spread):
        gap = mean - other
        return (mean + other) * 0.5, spread + other_spread + gap * gap * (0.5 * count)

    for step in (4, 2, 1):
        mean, spread = join(mean, spread, pltpu.roll(mean, step, 0), pltpu.roll(spread, step, 0))
        count *= 2.0
    step = 1
    while step < width:
        mean, spread = join(mean, spread, lane_partner(mean, step), lane_partner(spread, step))
        count *= 2.0
        step *= 2
    return mean, lax.rsqrt(spread * (1.0 / count) + EPS)


def side(frame, cols, step):
    lines = frame.reshape(-1, cols, frame.shape[1])
    moved = pltpu.roll(lines, (-step) % cols, 1)
    col = lax.broadcasted_iota(jnp.int32, lines.shape, 1)
    keep = col < cols - 1 if step > 0 else col > 0
    return jnp.where(keep, moved, 0.0).reshape(frame.shape)


def row_shift(frame, cols, step):
    gap = jnp.zeros((cols, frame.shape[1]), frame.dtype)
    if step > 0:
        return jnp.concatenate([frame[cols:], gap], axis=0)
    return jnp.concatenate([gap, frame[:-cols]], axis=0)


def three_rows(frame, cols, steps):
    return [(frame if step == 0 else row_shift(frame, cols, step)).astype(BF) for step in steps]


def put_rows(spread, index, a, pieces):
    for b, piece in enumerate(pieces):
        chans = piece.shape[1]
        at = (3 * a + b) * chans
        spread[index, :, at : at + chans] = piece


def join_cols(parts, cols, chans, steps):
    total = None
    for at, step in enumerate(steps):
        piece = parts[:, at * chans : (at + 1) * chans]
        piece = piece if step == 0 else side(piece, cols, step)
        total = piece if total is None else total + piece
    return total


def copies_of(chunks, halves, target, sem):
    quarter = chunks[0].shape[1]
    return [
        pltpu.make_async_copy(
            ref.at[0 : target.shape[0]], target.at[:, pl.ds(pl.multiple_of(at * quarter, quarter), quarter), :], sem
        )
        for ref, at in zip(chunks, halves)
    ]


def piece_ids(ids, n_chunk):
    per = n_chunk // 2
    return [ids[1] * per + j for j in range(per)] + [(1 - ids[1]) * per + j for j in range(per)]


def forward_matrix(taps):
    chans = taps.shape[-1]
    parts = taps.reshape(9, 3, chans, chans)
    return jnp.concatenate([parts[:, c].reshape(9 * chans, chans) for c in range(3)], axis=1)


def backward_matrix(taps):
    chans = taps.shape[-1]
    parts = taps.reshape(9, 3 * chans, chans)
    return jnp.concatenate([parts[ab] for ab in range(9)], axis=1)


def norm_parts(x32, mean, rstd, gain):
    normed = (x32 - mean) * rstd
    scaled = normed * gain
    return normed, scaled, 0.5 * jnp.tanh(0.5 * scaled) + 0.5


def full(row, count):
    return jnp.broadcast_to(row[:1], (count, row.shape[1]))


def spread_forward(dims, values, found, gain, spread):
    frames, rows, cols, chans = dims
    plane, points = rows * cols, frames * rows * cols
    for k, x32 in enumerate(values):
        mean, rstd = found[k]
        _, scaled, gate = norm_parts(x32, full(mean, points), full(rstd, points), full(gain, points))
        act = scaled * gate
        for source in range(frames):
            pieces = three_rows(act[source * plane : (source + 1) * plane], cols, (-1, 0, 1))
            for f in range(frames):
                for a in range(3):
                    if max(f - 2 + a, 0) == source:
                        put_rows(spread, k * frames + f, a, pieces)


def cut_kernel(parts, ids, gain, own, *refs):
    pieces, sems = refs[:parts], refs[parts]
    taps, quarter = own.shape[0], pieces[0].shape[1]
    copies = []
    for j in range(parts):
        rows = pl.ds(pl.multiple_of((ids[1] * parts + j) * quarter, quarter), quarter)
        copies.append(pltpu.make_async_copy(own.at[:, rows, :], pieces[j].at[0:taps], sems.at[j]))
    for copy in copies:
        copy.start()
    wide = full(gain[...], quarter)
    high = wide.astype(BF).astype(F32)
    middle = (wide - high).astype(BF).astype(F32)
    low = wide - high - middle
    row = lax.broadcasted_iota(jnp.int32, wide.shape, 0)
    pieces[0][taps] = jnp.where(row == 0, high, jnp.where(row == 1, middle, low)).astype(BF)
    for copy in copies:
        copy.wait()


def forward_kernel(sections, dims, ids, x_ref, gain, *refs):
    frames, rows, cols, chans = dims
    plane = rows * cols
    n_chunk = (len(refs) - 9 - sections) // sections
    chunks = [refs[k * n_chunk : (k + 1) * n_chunk] for k in range(sections)]
    refs = refs[sections * n_chunk :]
    outs, stats, every = refs[:3]
    sends = refs[3 : 3 + sections]
    spread, product, inputs, gain_rows, gain_sem, sems = refs[3 + sections :]
    place = ids[0]
    taps = every.shape[1]
    copies = [
        pltpu.make_async_copy(chunks[k][0].at[taps], gain_rows.at[k - 1], gain_sem.at[k - 1])
        for k in range(1, sections)
    ]
    for copy in copies:
        copy.start()

    for k in range(sections):
        for copy in copies_of(chunks[k], piece_ids(ids, n_chunk), every.at[k], sems.at[k]):
            copy.start()
    stats[place, 16:24] = full(gain[...], 8)
    for k in range(1, sections):
        copies[k - 1].wait()
        parts = gain_rows[k - 1].astype(F32)
        stats[place ^ k, 16:24] = full(parts[0:1] + parts[1:2] + parts[2:3], 8)
    x = x_ref[...]
    for unit in range(sections):
        inputs[unit] = x
        x32 = x.astype(F32)
        mean, rstd = statistics(x32, chans // GROUPS)
        stats[unit, 0:8], stats[unit, 8:16] = mean, rstd
        spread_forward(dims, [x32], [(mean, rstd)], stats[unit, 16:17], spread)
        source = place ^ unit
        pltpu.make_async_copy(every.at[source], every.at[source], sems.at[source]).wait()
        lhs = spread[...].reshape(frames * plane, 9 * chans)
        product[...] = jnp.dot(lhs, forward_matrix(every[source]), preferred_element_type=F32)
        for f in range(frames):
            spot = slice(f * plane, (f + 1) * plane)
            joined = join_cols(product[spot], cols, chans, (-1, 0, 1))
            outs[unit, spot] = (x32[spot] + joined).astype(BF)
        x = outs[unit]
    for k in range(sections):
        sends[k][...] = inputs[place ^ k]


def turn_kernel(dims, n, gain, *refs):
    frames, rows, cols, chans = dims
    plane, points = rows * cols, frames * rows * cols
    xs, (turned, stats) = refs[:n], refs[n:]
    for k in range(n):
        x32 = xs[k][...].astype(F32)
        mean, rstd = statistics(x32, chans // GROUPS)
        stats[k, 0:8], stats[k, 8:16] = mean, rstd
        _, scaled, gate = norm_parts(x32, full(mean, points), full(rstd, points), full(gain[...], points))
        act = (scaled * gate).astype(BF).astype(F32)
        for f in range(frames):
            frame = act[f * plane : (f + 1) * plane]
            for at, step in enumerate((-1, 0, 1)):
                piece = frame if step == 0 else side(frame, cols, step)
                turned[at * chans : (at + 1) * chans, pl.ds((f * n + k) * plane, plane)] = piece.T.astype(BF)


def home_forward_kernel(dims, n, ids, stats, gain, own, *refs):
    frames, rows, cols, chans = dims
    plane = rows * cols
    xs, (seg, spread) = refs[:n], refs[n:]
    values = [ref[...].astype(F32) for ref in xs]
    known = [(stats[k, 0:8], stats[k, 8:16]) for k in range(n)]
    spread_forward(dims, values, known, gain[...], spread)
    lhs = spread[...].reshape(n * frames * plane, 9 * chans)
    product = jnp.dot(lhs, forward_matrix(own[...]), preferred_element_type=F32)
    for k in range(n):
        at = (ids[0] ^ k) % n
        for f in range(frames):
            spot = slice(f * plane, (f + 1) * plane)
            joined = join_cols(product[(k * frames + f) * plane : (k * frames + f + 1) * plane], cols, chans, (-1, 0, 1))
            seg[at, spot] = (values[k][spot] + joined).astype(BF)


def unit_backward(dims, x32, grad, stat, gain, multiply, spread):
    frames, rows, cols, chans = dims
    plane, points = rows * cols, frames * rows * cols
    width = chans // GROUPS
    count = float(points * width)
    g32 = grad.astype(F32)
    per = [g32[f * plane : (f + 1) * plane] for f in range(frames)]
    for f in range(frames):
        for a in range(3):
            sources = [q for q in range(frames) if max(q - 2 + a, 0) == f]
            if sources:
                total = functools.reduce(lambda u, v: u + v, [per[q] for q in sources])
                put_rows(spread, f, a, three_rows(total, cols, (1, 0, -1)))
            else:
                put_rows(spread, f, a, [jnp.zeros((plane, chans), BF)] * 3)
    product = multiply(spread[...].reshape(points, 9 * chans))
    gact = jnp.concatenate(
        [join_cols(product[f * plane : (f + 1) * plane], cols, chans, (1, 0, -1)) for f in range(frames)], axis=0
    )
    rstd = full(stat[8:16], points)
    wide_gain = full(gain, points)
    normed, scaled, gate = norm_parts(x32, full(stat[0:8], points), rstd, wide_gain)
    d_normed = gact * (gate * (1.0 + scaled * (1.0 - gate))) * wide_gain
    m1 = group_sum(d_normed, width) * (1.0 / count)
    m2 = group_sum(d_normed * normed, width) * (1.0 / count)
    dx = rstd * (d_normed - full(m1, points) - normed * full(m2, points))
    return (g32 + dx).astype(BF)


def times_transposed(lhs, taps):
    return lax.dot_general(lhs, backward_matrix(taps), (((1,), (1,)), ((), ())), preferred_element_type=F32)


def backward_kernel(sections, dims, ids, outs, grad_ref, stats, every, *refs):
    sends, (spread, grads) = refs[:sections], refs[sections:]
    place = ids[0]
    grad = grad_ref[...]
    grads[sections - 1] = grad
    for unit in range(sections - 1, 0, -1):

        def multiply(lhs, unit=unit):
            return times_transposed(lhs, every[place ^ unit])

        grad = unit_backward(dims, outs[unit - 1].astype(F32), grad, stats[unit], stats[unit, 16:17], multiply, spread)
        grads[unit - 1] = grad
    for k in range(sections):
        sends[k][...] = grads[place ^ k]


def home_backward_kernel(dims, n, first, last, ids, stats, gain, own, *refs):
    count = last - first
    xs, grads = refs[:count], refs[count : 2 * count]
    refs = refs[2 * count :]
    done = refs[:first] if last == n else ()
    outs, spread = refs[len(done) : -1], refs[-1]
    place = ids[0]
    for k in range(len(done)):
        outs[0][(place ^ k) % n] = done[k][...]
    for i in range(count):
        result = unit_backward(
            dims,
            xs[i][...].astype(F32),
            grads[i][...],
            stats[first + i],
            gain[...],
            lambda lhs: times_transposed(lhs, own[...]),
            spread,
        )
        if last == n:
            outs[0][(place ^ (first + i)) % n] = result
        else:
            outs[i][...] = result


def tap_spots(frames, n, plane):
    spots = [0]
    for a in range(3):
        spots.append(spots[-1] + max(1, frames - 2 + a) * n * plane)
    return spots


def put_right(dims, n, grads, right):
    frames, rows, cols, chans = dims
    plane = rows * cols
    spots = tap_spots(frames, n, plane)
    for k in range(n):
        mine = grads[k][...].astype(F32)
        per = [mine[f * plane : (f + 1) * plane] for f in range(frames)]
        for a in range(3):
            folded = [f for f in range(frames) if f - 2 + a <= 0]
            groups = [folded] + [[f] for f in range(frames) if f - 2 + a > 0]
            for i, group in enumerate(groups):
                total = functools.reduce(lambda u, v: u + v, [per[f] for f in group])
                at = spots[a] + (i * n + k) * plane
                for b, piece in enumerate(three_rows(total, cols, (1, 0, -1))):
                    right[at : at + plane, b * chans : (b + 1) * chans] = piece


def put_term(dims, n, a, taps, turned, right, term, base):
    frames, rows, cols, chans = dims
    spots = tap_spots(frames, n, rows * cols)
    used = spots[a + 1] - spots[a]
    rhs = right[spots[a] : spots[a + 1], taps[0] * chans : (taps[-1] + 1) * chans]
    out = jnp.dot(turned[:, 0:used], rhs, preferred_element_type=F32)
    for b in range(len(taps)):
        for c in range(3):
            block = out[c * chans : (c + 1) * chans, b * chans : (b + 1) * chans]
            term[pl.ds(base + (b * 3 + c) * chans, chans), :] = block.astype(BF)


def term_kernel(dims, n, turned, *refs):
    grads, (term, right) = refs[:n], refs[n:]
    put_right(dims, n, grads, right)
    for a in range(3):
        put_term(dims, n, a, (0, 1, 2), turned, right, term, a * 9 * dims[3])


def half_kernel(dims, n, far, levels, ids, turned, *refs):
    chans = dims[3]
    if far:
        put_right(dims, n, refs[:n], refs[n])
        refs = refs[n:]
    right, keep, send, term = refs
    upper = ids[2] >= levels // 2

    def low():
        put_term(dims, n, 0, (0, 1, 2), turned, right, term, 0)
        put_term(dims, n, 1, (0, 1), turned, right, term, 9 * chans)

    def high():
        put_term(dims, n, 1, (1, 2), turned, right, term, 0)
        put_term(dims, n, 2, (0, 1, 2), turned, right, term, 6 * chans)

    wants_high = jnp.logical_not(upper) if far else upper
    pl.when(wants_high)(high)
    pl.when(jnp.logical_not(wants_high))(low)
    skip = jnp.where(wants_high, 27 * chans // 2 - 12 * chans, 0)
    core = ids[1]
    size = keep.shape[1]
    for j in range(levels // 2):
        here = pl.multiple_of(skip + (2 * j + core) * size, 16)
        there = pl.multiple_of(skip + (2 * j + 1 - core) * size, 16)
        keep[j] = term[pl.ds(here, size), :]
        send[j] = term[pl.ds(there, size), :]


def pair_kernel(distances, ids, keep, got, *sends):
    for k, out in zip(distances, sends):
        at = lax.rem(ids[2] ^ k, keep.shape[0])
        out[...] = (keep[at].astype(F32) + got[at].astype(F32)).astype(out.dtype)


def sum_kernel(scale, own, *refs):
    total = own[...]
    for ref in refs[:-1]:
        total = total + ref[...].astype(F32)
    refs[-1][...] = total * scale


def gather_chunks(mine, sections, ride):
    parts = len(mine)
    got = {}
    if sections == 4 and parts == 2:
        first = swap(mine[0], "pipe", 1)
        second = swap(mine[1], "pipe", 2)
        first, *ride = lax.optimization_barrier((first, *ride))
        got[1] = [first, swap(mine[1], "pipe", 1)]
        got[2] = [swap(mine[0], "pipe", 2), second]
        got[3] = [swap(first, "pipe", 2), swap(second, "pipe", 1)]
    else:
        for k in range(1, sections):
            got[k] = [swap(piece, "pipe", k) for piece in mine]
    return got, ride


def body(video, cotangent, weights, gains):
    sections = lax.axis_size("pipe")
    ranks = lax.axis_size("dp")
    place = lax.axis_index("pipe")
    rank = lax.axis_index("dp")
    core = lax.rem(rank, 2)
    micro, clips, frames, rows, cols, chans = video.shape
    ids = jnp.stack([place, core, lax.div(rank, 2)]).astype(jnp.int32)
    points = frames * rows * cols
    dims = (frames, rows, cols, chans)
    parts = 2
    n_chunk = 2 * parts
    quarter = chans // n_chunk

    video = video.reshape(micro, points, chans)
    cot = cotangent.reshape(micro, points, chans)
    kernel_rows = weights.reshape(27, chans, chans)
    gain_rows = jnp.broadcast_to(gains, (8, chans))
    mine = call(
        functools.partial(cut_kernel, parts),
        [jax.ShapeDtypeStruct((27 + (j == 0), quarter, chans), BF) for j in range(parts)],
        [SM, VM, ANY],
        [VM] * parts,
        [pltpu.SemaphoreType.DMA((parts,))],
    )(ids, gain_rows, kernel_rows)
    x = lax.dynamic_index_in_dim(video, lax.rem(place, micro), 0, False)
    grad = lax.dynamic_index_in_dim(cot, lax.rem(place, micro), 0, False)
    got, (x, grad) = gather_chunks(mine, sections, (x, grad))
    got[0] = list(mine)
    flat = [piece for k in range(sections) for piece in got[k] + [swap(piece, "dp", 1) for piece in got[k]]]

    act_shape = jax.ShapeDtypeStruct((points, chans), BF)
    unit_flops = 2 * points * 27 * chans * chans
    n = min(sections, micro)
    spots = sum(max(1, frames - 2 + a) for a in range(3))

    def spread(count):
        return pltpu.VMEM((count * frames, rows * cols, 9 * chans), BF)

    product = pltpu.VMEM((points, 3 * chans), F32)

    outs, stats, every, *xsends = call(
        functools.partial(forward_kernel, sections, dims),
        [
            jax.ShapeDtypeStruct((sections, points, chans), BF),
            jax.ShapeDtypeStruct((sections, 24, chans), F32),
            jax.ShapeDtypeStruct((sections, 27, chans, chans), BF),
        ]
        + [act_shape] * sections,
        [SM, VM, VM] + [ANY] * len(flat),
        [VM] * (3 + sections),
        [
            spread(1),
            product,
            pltpu.VMEM((sections, points, chans), BF),
            pltpu.VMEM((sections - 1, quarter, chans), BF),
            pltpu.SemaphoreType.DMA((sections - 1,)),
            pltpu.SemaphoreType.DMA((sections,)),
        ],
        flops=4 * sections * unit_flops,
    )(ids, x, gain_rows, *flat)
    xs_home = [xsends[0]] + [swap(xsends[k], "pipe", k) for k in range(1, n)]

    gsends = call(
        functools.partial(backward_kernel, sections, dims),
        [act_shape] * sections,
        [SM] + [VM] * 4,
        [VM] * sections,
        [spread(1), pltpu.VMEM((sections, points, chans), BF)],
        flops=4 * (sections - 1) * unit_flops,
    )(ids, outs, grad, stats, every)
    grads_home = [gsends[0]] + [swap(gsends[k], "pipe", k) for k in range(1, n)]

    turned, home_stats = call(
        functools.partial(turn_kernel, dims, n),
        [jax.ShapeDtypeStruct((3 * chans, n * points), BF), jax.ShapeDtypeStruct((n, 16, chans), F32)],
        [VM] * (1 + n),
        [VM] * 2,
        flops=n * unit_flops,
    )(gain_rows, *xs_home)

    def home_forward(ids):
        return call(
            functools.partial(home_forward_kernel, dims, n),
            jax.ShapeDtypeStruct((micro, points, chans), BF),
            [SM, VM, VM, VM] + [VM] * n,
            VM,
            [spread(n)],
            flops=4 * n * unit_flops,
        )(ids, home_stats, gain_rows, kernel_rows, *xs_home)

    def home_backward(first, last, done, ids):
        count = last - first
        return call(
            functools.partial(home_backward_kernel, dims, n, first, last),
            [jax.ShapeDtypeStruct((micro, points, chans), BF)] if last == n else [act_shape] * count,
            [SM, VM, VM, VM] + [VM] * (2 * count + len(done)),
            [VM] * (1 if last == n else count),
            [spread(1)],
            flops=4 * count * unit_flops,
        )(ids, home_stats, gain_rows, kernel_rows, *xs_home[first:last], *grads_home[first:last], *done)

    seg = home_forward(ids)
    turned, seg = lax.optimization_barrier((turned, seg))

    size = 27 * chans // ranks
    levels = ranks // 2
    right_shape = jax.ShapeDtypeStruct((tap_spots(frames, n, rows * cols)[-1], 3 * chans), BF)

    def pair(keep, got, distances):
        return call(
            functools.partial(pair_kernel, distances),
            [jax.ShapeDtypeStruct((size, chans), BF if k else F32) for k in distances],
            [SM, VM, VM],
            [VM] * len(distances),
        )(ids, keep, got)

    if size % 16 == 0 and levels % 2 == 0:
        half = [jax.ShapeDtypeStruct((levels // 2, size, chans), BF)] * 2
        term = pltpu.VMEM((15 * chans, chans), BF)
        right, keep, send = call(
            functools.partial(half_kernel, dims, n, True, levels),
            [right_shape] + half,
            [SM, VM] + [VM] * n,
            [VM] * 3,
            [term],
            flops=n * unit_flops // 2,
        )(ids, turned, *grads_home)
        got = swap(send, "dp", 1)
        near_keep, near_send = call(
            functools.partial(half_kernel, dims, n, False, levels),
            half,
            [SM, VM, VM],
            [VM] * 2,
            [term],
            flops=n * unit_flops // 2,
        )(ids, turned, right)
        near_send, got = lax.optimization_barrier((near_send, got))
        near_got = swap(near_send, "dp", 1)
        far = range(levels // 2, levels)
        zsends = dict(zip(far, pair(keep, got, far)))
        near = range(levels // 2)
        zsends.update(zip(near, pair(near_keep, near_got, near)))
    else:
        term = call(
            functools.partial(term_kernel, dims, n),
            jax.ShapeDtypeStruct((27 * chans, chans), BF),
            [VM] * (1 + n),
            VM,
            [pltpu.VMEM(right_shape.shape, BF)],
            flops=n * unit_flops,
        )(turned, *grads_home)
        shares = term.reshape(levels, 2, size, chans)
        keep = lax.dynamic_index_in_dim(shares, core, 1, False)
        got = swap(lax.dynamic_index_in_dim(shares, 1 - core, 1, False), "dp", 1)
        zsends = dict(enumerate(pair(keep, got, range(levels))))
    own = zsends[0]
    arrived = [swap(zsends[k], "dp", 2 * k) for k in (*range(levels // 2, levels), *range(1, levels // 2))]

    late, own = lax.optimization_barrier((ids, own))
    (ing,) = home_backward(0, n, (), late)

    scale = 1.0 / math.sqrt(micro * clips * ranks * points)
    share = call(
        functools.partial(sum_kernel, scale),
        jax.ShapeDtypeStruct((size, chans), F32),
        [VM] * levels,
        VM,
    )(own, *arrived)

    shape = (1, micro, clips, frames, rows, cols, chans)
    return (seg.reshape(shape), ing.reshape(shape), share.reshape(1, size * chans))


def solution(mesh):
    in_specs = (
        P(None, "dp", None, None, None, None),
        P(None, "dp", None, None, None, None),
        P("pipe", None, None),
        P("pipe", None),
    )
    out_specs = (
        P("pipe", None, "dp", None, None, None, None),
        P("pipe", None, "dp", None, None, None, None),
        P("pipe", "dp"),
    )
    return jax.shard_map(body, mesh=mesh, in_specs=in_specs, out_specs=out_specs, check_vma=False)
```

```python
import functools
import math

import jax
import jax.numpy as jnp
from jax import lax
from jax.experimental import pallas as pl
from jax.experimental.pallas import tpu as pltpu
from jax.sharding import PartitionSpec as P

GROUPS = 32
EPS = 1e-06
BF, F32 = jnp.bfloat16, jnp.float32
VMEM_LIMIT = 28 * 1024 * 1024
VM = pl.BlockSpec(memory_space=pltpu.VMEM)
SM = pl.BlockSpec(memory_space=pltpu.SMEM)
ANY = pl.BlockSpec(memory_space=pl.ANY)
HBM = pl.BlockSpec(memory_space=pltpu.HBM)


def call(kernel, out_shape, in_specs, out_specs, scratch=(), flops=0, moved=0, limit=VMEM_LIMIT):
    return pl.pallas_call(
        kernel,
        out_shape=out_shape,
        in_specs=in_specs,
        out_specs=out_specs,
        scratch_shapes=list(scratch),
        compiler_params=pltpu.CompilerParams(vmem_limit_bytes=limit),
        cost_estimate=pl.CostEstimate(flops=flops, bytes_accessed=moved, transcendentals=0),
    )


def swap(value, axis, bits):
    count = lax.axis_size(axis)
    return lax.ppermute(value, axis, [(i, i ^ bits) for i in range(count)])


def lane_partner(row, step):
    lane = lax.broadcasted_iota(jnp.int32, row.shape, 1)
    ahead = pltpu.roll(row, row.shape[1] - step, 1)
    return jnp.where((lane & step) == 0, ahead, pltpu.roll(row, step, 1))


def tree(parts):
    parts = list(parts)
    while len(parts) > 1:
        pairs = [u + v for u, v in zip(parts[::2], parts[1::2])]
        parts = pairs + parts[len(pairs) * 2 :]
    return parts[0]


def tiles(values):
    return [values[i : i + 8] for i in range(0, values.shape[0], 8)]


def group_sum(values, width):
    row = tree(tiles(values))
    for step in (4, 2, 1):
        row = row + pltpu.roll(row, step, 0)
    step = 1
    while step < width:
        row = row + lane_partner(row, step)
        step *= 2
    return row


def statistics(x32, width):
    parts = tiles(x32)
    pivot = parts[0]
    gaps = [part - pivot for part in parts[1:]]
    first = tree(gaps)
    second = tree([gap * gap for gap in gaps])
    count = float(len(parts))
    mean = pivot + first * (1.0 / count)
    spread = jnp.maximum(second - first * first * (1.0 / count), 0.0)

    def join(mean, spread, other, other_spread):
        gap = mean - other
        return (mean + other) * 0.5, spread + other_spread + gap * gap * (0.5 * count)

    for step in (4, 2, 1):
        mean, spread = join(mean, spread, pltpu.roll(mean, step, 0), pltpu.roll(spread, step, 0))
        count *= 2.0
    step = 1
    while step < width:
        mean, spread = join(mean, spread, lane_partner(mean, step), lane_partner(spread, step))
        count *= 2.0
        step *= 2
    return mean, lax.rsqrt(spread * (1.0 / count) + EPS)


def side(frame, cols, step):
    lines = frame.reshape(-1, cols, frame.shape[1])
    moved = pltpu.roll(lines, (-step) % cols, 1)
    col = lax.broadcasted_iota(jnp.int32, lines.shape, 1)
    keep = col < cols - 1 if step > 0 else col > 0
    return jnp.where(keep, moved, 0.0).reshape(frame.shape)


def row_shift(frame, cols, step):
    gap = jnp.zeros((cols, frame.shape[1]), frame.dtype)
    if step > 0:
        return jnp.concatenate([frame[cols:], gap], axis=0)
    return jnp.concatenate([gap, frame[:-cols]], axis=0)


def three_rows(frame, cols, steps):
    return [(frame if step == 0 else row_shift(frame, cols, step)).astype(BF) for step in steps]


def put_rows(spread, index, a, pieces):
    for b, piece in enumerate(pieces):
        chans = piece.shape[1]
        at = (3 * a + b) * chans
        spread[index, :, at : at + chans] = piece


def join_cols(parts, cols, chans, steps):
    total = None
    for at, step in enumerate(steps):
        piece = parts[:, at * chans : (at + 1) * chans]
        piece = piece if step == 0 else side(piece, cols, step)
        total = piece if total is None else total + piece
    return total


def copies_of(chunks, halves, target, sem):
    quarter = chunks[0].shape[1]
    return [
        pltpu.make_async_copy(
            ref.at[0 : target.shape[0]], target.at[:, pl.ds(pl.multiple_of(at * quarter, quarter), quarter), :], sem
        )
        for ref, at in zip(chunks, halves)
    ]


def piece_ids(ids, n_chunk):
    per = n_chunk // 2
    return [ids[1] * per + j for j in range(per)] + [(1 - ids[1]) * per + j for j in range(per)]


def forward_matrix(taps):
    chans = taps.shape[-1]
    parts = taps.reshape(9, 3, chans, chans)
    return jnp.concatenate([parts[:, c].reshape(9 * chans, chans) for c in range(3)], axis=1)


def backward_matrix(taps):
    chans = taps.shape[-1]
    parts = taps.reshape(9, 3 * chans, chans)
    return jnp.concatenate([parts[ab] for ab in range(9)], axis=1)


def norm_parts(x32, mean, rstd, gain):
    normed = (x32 - mean) * rstd
    scaled = normed * gain
    return normed, scaled, 0.5 * jnp.tanh(0.5 * scaled) + 0.5


def full(row, count):
    return jnp.broadcast_to(row[:1], (count, row.shape[1]))


def spread_forward(dims, values, found, gain, spread):
    frames, rows, cols, chans = dims
    plane, points = rows * cols, frames * rows * cols
    for k, x32 in enumerate(values):
        mean, rstd = found[k]
        _, scaled, gate = norm_parts(x32, full(mean, points), full(rstd, points), full(gain, points))
        act = scaled * gate
        for source in range(frames):
            pieces = three_rows(act[source * plane : (source + 1) * plane], cols, (-1, 0, 1))
            for f in range(frames):
                for a in range(3):
                    if max(f - 2 + a, 0) == source:
                        put_rows(spread, k * frames + f, a, pieces)


def forward_kernel(sections, dims, ids, x_ref, *refs):
    frames, rows, cols, chans = dims
    plane = rows * cols
    n_chunk = (len(refs) - 9 - sections) // sections
    chunks = [refs[k * n_chunk : (k + 1) * n_chunk] for k in range(sections)]
    refs = refs[sections * n_chunk :]
    outs, stats, every = refs[:3]
    sends = refs[3 : 3 + sections]
    spread, product, inputs, gains, gain_sem, sems = refs[3 + sections :]
    place = ids[0]
    taps = every.shape[1]
    copies = [
        pltpu.make_async_copy(chunks[k][0].at[taps], gains.at[k], gain_sem.at[k])
        for k in range(sections)
    ]
    for copy in copies:
        copy.start()

    for k in range(sections):
        for copy in copies_of(chunks[k], piece_ids(ids, n_chunk), every.at[k], sems.at[k]):
            copy.start()
    for k in range(sections):
        copies[k].wait()
        parts = gains[k].astype(F32)
        stats[place ^ k, 16:24] = full(parts[0:1] + parts[1:2] + parts[2:3], 8)
    x = x_ref[...]
    for unit in range(sections):
        inputs[unit] = x
        x32 = x.astype(F32)
        mean, rstd = statistics(x32, chans // GROUPS)
        stats[unit, 0:8], stats[unit, 8:16] = mean, rstd
        spread_forward(dims, [x32], [(mean, rstd)], stats[unit, 16:17], spread)
        source = place ^ unit
        pltpu.make_async_copy(every.at[source], every.at[source], sems.at[source]).wait()
        lhs = spread[...].reshape(frames * plane, 9 * chans)
        product[...] = jnp.dot(lhs, forward_matrix(every[source]), preferred_element_type=F32)
        for f in range(frames):
            spot = slice(f * plane, (f + 1) * plane)
            joined = join_cols(product[spot], cols, chans, (-1, 0, 1))
            outs[unit, spot] = (x32[spot] + joined).astype(BF)
        x = outs[unit]
    for k in range(sections):
        sends[k][...] = inputs[place ^ k]


def turn_kernel(dims, n, ids, unit_stats, *refs):
    frames, rows, cols, chans = dims
    plane, points = rows * cols, frames * rows * cols
    xs, (turned, stats) = refs[:n], refs[n:]
    gain = unit_stats[ids[0], 16:24]
    for k in range(n):
        x32 = xs[k][...].astype(F32)
        mean, rstd = statistics(x32, chans // GROUPS)
        stats[k, 0:8], stats[k, 8:16], stats[k, 16:24] = mean, rstd, gain
        _, scaled, gate = norm_parts(x32, full(mean, points), full(rstd, points), full(gain, points))
        act = (scaled * gate).astype(BF).astype(F32)
        for f in range(frames):
            frame = act[f * plane : (f + 1) * plane]
            for at, step in enumerate((-1, 0, 1)):
                piece = frame if step == 0 else side(frame, cols, step)
                turned[at * chans : (at + 1) * chans, pl.ds((f * n + k) * plane, plane)] = piece.T.astype(BF)


def home_forward_kernel(dims, n, first, last, ids, stats, own, *refs):
    frames, rows, cols, chans = dims
    plane = rows * cols
    count = last - first
    xs, refs = refs[:count], refs[count:]
    done = refs[:first] if last == n else ()
    outs, spread = refs[len(done) : -1], refs[-1]
    for k in range(len(done)):
        outs[0][lax.rem(ids[0] ^ k, n)] = done[k][...]
    values = [ref[...].astype(F32) for ref in xs]
    known = [(stats[first + i, 0:8], stats[first + i, 8:16]) for i in range(count)]
    spread_forward(dims, values, known, stats[0, 16:17], spread)
    lhs = spread[...].reshape(count * frames * plane, 9 * chans)
    product = jnp.dot(lhs, forward_matrix(own[...]), preferred_element_type=F32)
    for i in range(count):
        at = lax.rem(ids[0] ^ (first + i), n)
        for f in range(frames):
            spot = slice(f * plane, (f + 1) * plane)
            joined = join_cols(product[(i * frames + f) * plane : (i * frames + f + 1) * plane], cols, chans, (-1, 0, 1))
            result = (values[i][spot] + joined).astype(BF)
            if last == n:
                outs[0][at, spot] = result
            else:
                outs[i][spot] = result


def unit_backward(dims, x32, grad, stat, gain, multiply, spread):
    frames, rows, cols, chans = dims
    plane, points = rows * cols, frames * rows * cols
    width = chans // GROUPS
    count = float(points * width)
    g32 = grad.astype(F32)
    per = [g32[f * plane : (f + 1) * plane] for f in range(frames)]
    for f in range(frames):
        for a in range(3):
            sources = [q for q in range(frames) if max(q - 2 + a, 0) == f]
            if sources:
                total = functools.reduce(lambda u, v: u + v, [per[q] for q in sources])
                put_rows(spread, f, a, three_rows(total, cols, (1, 0, -1)))
            else:
                put_rows(spread, f, a, [jnp.zeros((plane, chans), BF)] * 3)
    product = multiply(spread[...].reshape(points, 9 * chans))
    gact = jnp.concatenate(
        [join_cols(product[f * plane : (f + 1) * plane], cols, chans, (1, 0, -1)) for f in range(frames)], axis=0
    )
    rstd = full(stat[8:16], points)
    wide_gain = full(gain, points)
    normed, scaled, gate = norm_parts(x32, full(stat[0:8], points), rstd, wide_gain)
    d_normed = gact * (gate * (1.0 + scaled * (1.0 - gate))) * wide_gain
    m1 = group_sum(d_normed, width) * (1.0 / count)
    m2 = group_sum(d_normed * normed, width) * (1.0 / count)
    dx = rstd * (d_normed - full(m1, points) - normed * full(m2, points))
    return (g32 + dx).astype(BF)


def times_transposed(lhs, taps):
    return lax.dot_general(lhs, backward_matrix(taps), (((1,), (1,)), ((), ())), preferred_element_type=F32)


def backward_kernel(sections, dims, ids, outs, grad_ref, stats, every, *refs):
    sends, (spread, grads) = refs[:sections], refs[sections:]
    place = ids[0]
    grad = grad_ref[...]
    grads[sections - 1] = grad
    for unit in range(sections - 1, 0, -1):

        def multiply(lhs, unit=unit):
            return times_transposed(lhs, every[place ^ unit])

        grad = unit_backward(dims, outs[unit - 1].astype(F32), grad, stats[unit], stats[unit, 16:17], multiply, spread)
        grads[unit - 1] = grad
    for k in range(sections):
        sends[k][...] = grads[place ^ k]


def home_backward_kernel(dims, n, first, last, ids, stats, own, *refs):
    count = last - first
    xs, grads = refs[:count], refs[count : 2 * count]
    refs = refs[2 * count :]
    done = refs[:first] if last == n else ()
    outs, spread = refs[len(done) : -1], refs[-1]
    place = ids[0]
    for k in range(len(done)):
        outs[0][(place ^ k) % n] = done[k][...]
    for i in range(count):
        result = unit_backward(
            dims,
            xs[i][...].astype(F32),
            grads[i][...],
            stats[first + i],
            stats[0, 16:17],
            lambda lhs: times_transposed(lhs, own[...]),
            spread,
        )
        if last == n:
            outs[0][(place ^ (first + i)) % n] = result
        else:
            outs[i][...] = result


def tap_spots(frames, n, plane):
    spots = [0]
    for a in range(3):
        spots.append(spots[-1] + max(1, frames - 2 + a) * n * plane)
    return spots


def put_right(dims, n, grads, right):
    frames, rows, cols, chans = dims
    plane = rows * cols
    spots = tap_spots(frames, n, plane)
    for k in range(n):
        mine = grads[k][...].astype(F32)
        per = [mine[f * plane : (f + 1) * plane] for f in range(frames)]
        for a in range(3):
            folded = [f for f in range(frames) if f - 2 + a <= 0]
            groups = [folded] + [[f] for f in range(frames) if f - 2 + a > 0]
            for i, group in enumerate(groups):
                total = functools.reduce(lambda u, v: u + v, [per[f] for f in group])
                at = spots[a] + (i * n + k) * plane
                for b, piece in enumerate(three_rows(total, cols, (1, 0, -1))):
                    right[at : at + plane, b * chans : (b + 1) * chans] = piece


def put_term(dims, n, a, taps, turned, right, term, base):
    frames, rows, cols, chans = dims
    spots = tap_spots(frames, n, rows * cols)
    used = spots[a + 1] - spots[a]
    rhs = right[spots[a] : spots[a + 1], taps[0] * chans : (taps[-1] + 1) * chans]
    out = jnp.dot(turned[:, 0:used], rhs, preferred_element_type=F32)
    for b in range(len(taps)):
        for c in range(3):
            block = out[c * chans : (c + 1) * chans, b * chans : (b + 1) * chans]
            term[pl.ds(base + (b * 3 + c) * chans, chans), :] = block.astype(BF)


def term_kernel(dims, n, turned, *refs):
    grads, (term, right) = refs[:n], refs[n:]
    put_right(dims, n, grads, right)
    for a in range(3):
        put_term(dims, n, a, (0, 1, 2), turned, right, term, a * 9 * dims[3])


def half_kernel(dims, n, far, levels, ids, turned, *refs):
    chans = dims[3]
    if far:
        put_right(dims, n, refs[:n][::-1], refs[n])
        refs = refs[n:]
    right, keep, send, term = refs
    upper = ids[2] >= levels // 2

    def low():
        put_term(dims, n, 0, (0, 1, 2), turned, right, term, 0)
        put_term(dims, n, 1, (0, 1), turned, right, term, 9 * chans)

    def high():
        put_term(dims, n, 1, (1, 2), turned, right, term, 0)
        put_term(dims, n, 2, (0, 1, 2), turned, right, term, 6 * chans)

    wants_high = jnp.logical_not(upper) if far else upper
    pl.when(wants_high)(high)
    pl.when(jnp.logical_not(wants_high))(low)
    skip = jnp.where(wants_high, 27 * chans // 2 - 12 * chans, 0)
    core = ids[1]
    size = keep.shape[1]
    for j in range(levels // 2):
        here = pl.multiple_of(skip + (2 * j + core) * size, 16)
        there = pl.multiple_of(skip + (2 * j + 1 - core) * size, 16)
        keep[j] = term[pl.ds(here, size), :]
        send[j] = term[pl.ds(there, size), :]


def pair_kernel(distances, ids, keep, got, *sends):
    for k, out in zip(distances, sends):
        at = lax.rem(ids[2] ^ k, keep.shape[0])
        out[...] = (keep[at].astype(F32) + got[at].astype(F32)).astype(out.dtype)


def sum_kernel(scale, own, *refs):
    total = own[...]
    for ref in refs[:-1]:
        total = total + ref[...].astype(F32)
    refs[-1][...] = total * scale


def with_gains(piece, gains):
    taps, rows, chans = piece.shape
    high = lax.reduce_precision(gains, 8, 7)
    middle = lax.reduce_precision(gains - high, 8, 7)
    low = gains - high - middle
    shape = (taps + 1, rows, chans)
    row = lax.broadcasted_iota(jnp.int32, shape, 1)
    extra = jnp.where(row == 0, high[None], jnp.where(row == 1, middle[None], low[None])).astype(BF)
    padded = lax.pad(piece, jnp.zeros((), BF), ((0, 1, 0), (0, 0, 0), (0, 0, 0)))
    return jnp.where(lax.broadcasted_iota(jnp.int32, shape, 0) < taps, padded, extra)


def gather_chunks(mine, sections, ride):
    parts = len(mine)
    got = {}
    if sections == 4 and parts == 2:
        first = swap(mine[0], "pipe", 1)
        second = swap(mine[1], "pipe", 2)
        first, *ride = lax.optimization_barrier((first, *ride))
        got[1] = [first, swap(mine[1], "pipe", 1)]
        got[2] = [swap(mine[0], "pipe", 2), second]
        got[3] = [swap(first, "pipe", 2), swap(second, "pipe", 1)]
    else:
        for k in range(1, sections):
            got[k] = [swap(piece, "pipe", k) for piece in mine]
    return got, ride


def body(video, cotangent, weights, gains):
    sections = lax.axis_size("pipe")
    ranks = lax.axis_size("dp")
    place = lax.axis_index("pipe")
    rank = lax.axis_index("dp")
    core = lax.rem(rank, 2)
    micro, clips, frames, rows, cols, chans = video.shape
    ids = jnp.stack([place, core, lax.div(rank, 2)]).astype(jnp.int32)
    points = frames * rows * cols
    dims = (frames, rows, cols, chans)
    parts = 2
    n_chunk = 2 * parts
    quarter = chans // n_chunk

    video = video.reshape(micro, points, chans)
    cot = cotangent.reshape(micro, points, chans)
    kernel_rows = weights.reshape(27, chans, chans)
    cut = kernel_rows.reshape(27, n_chunk, quarter, chans)
    mine = [lax.dynamic_index_in_dim(cut, core * parts + j, 1, False) for j in range(parts)]
    mine[0] = with_gains(mine[0], gains)
    x = lax.dynamic_index_in_dim(video, lax.rem(place, micro), 0, False)
    grad = lax.dynamic_index_in_dim(cot, lax.rem(place, micro), 0, False)
    got, (x, grad) = gather_chunks(mine, sections, (x, grad))
    got[0] = list(mine)
    flat = [piece for k in range(sections) for piece in got[k] + [swap(piece, "dp", 1) for piece in got[k]]]

    act_shape = jax.ShapeDtypeStruct((points, chans), BF)
    unit_flops = 2 * points * 27 * chans * chans
    n = min(sections, micro)
    spots = sum(max(1, frames - 2 + a) for a in range(3))

    def spread(count):
        return pltpu.VMEM((count * frames, rows * cols, 9 * chans), BF)

    product = pltpu.VMEM((points, 3 * chans), F32)

    outs, stats, every, *xsends = call(
        functools.partial(forward_kernel, sections, dims),
        [
            jax.ShapeDtypeStruct((sections, points, chans), BF),
            jax.ShapeDtypeStruct((sections, 24, chans), F32),
            jax.ShapeDtypeStruct((sections, 27, chans, chans), BF),
        ]
        + [act_shape] * sections,
        [SM, VM] + [ANY] * len(flat),
        [VM] * (3 + sections),
        [
            spread(1),
            product,
            pltpu.VMEM((sections, points, chans), BF),
            pltpu.VMEM((sections, quarter, chans), BF),
            pltpu.SemaphoreType.DMA((sections,)),
            pltpu.SemaphoreType.DMA((sections,)),
        ],
        flops=4 * sections * unit_flops,
    )(ids, x, *flat)
    xs_home = [xsends[0]] + [swap(xsends[k], "pipe", k) for k in range(1, n)]

    gsends = call(
        functools.partial(backward_kernel, sections, dims),
        [act_shape] * sections,
        [SM] + [VM] * 4,
        [VM] * sections,
        [spread(1), pltpu.VMEM((sections, points, chans), BF)],
        flops=4 * (sections - 1) * unit_flops,
    )(ids, outs, grad, stats, every)
    grads_home = [gsends[0]] + [swap(gsends[k], "pipe", k) for k in range(1, n)]

    turned, home_stats = call(
        functools.partial(turn_kernel, dims, n),
        [jax.ShapeDtypeStruct((3 * chans, n * points), BF), jax.ShapeDtypeStruct((n, 24, chans), F32)],
        [SM] + [VM] * (1 + n),
        [VM] * 2,
        flops=n * unit_flops,
    )(ids, stats, *xs_home)

    def home_forward(first, last, done, ids):
        count = last - first
        return call(
            functools.partial(home_forward_kernel, dims, n, first, last),
            [jax.ShapeDtypeStruct((micro, points, chans), BF)] if last == n else [act_shape] * count,
            [SM, VM, VM] + [VM] * (count + len(done)),
            [VM] * (1 if last == n else count),
            [spread(count)],
            flops=4 * count * unit_flops,
        )(ids, home_stats, kernel_rows, *xs_home[first:last], *done)

    def home_backward(first, last, done, ids):
        count = last - first
        return call(
            functools.partial(home_backward_kernel, dims, n, first, last),
            [jax.ShapeDtypeStruct((micro, points, chans), BF)] if last == n else [act_shape] * count,
            [SM, VM, VM] + [VM] * (2 * count + len(done)),
            [VM] * (1 if last == n else count),
            [spread(1)],
            flops=4 * count * unit_flops,
        )(ids, home_stats, kernel_rows, *xs_home[first:last], *grads_home[first:last], *done)

    seg_early = home_forward(0, n // 2, (), ids)
    turned, *seg_early = lax.optimization_barrier((turned, *seg_early))

    size = 27 * chans // ranks
    levels = ranks // 2
    right_shape = jax.ShapeDtypeStruct((tap_spots(frames, n, rows * cols)[-1], 3 * chans), BF)

    def pair(keep, got, distances):
        return call(
            functools.partial(pair_kernel, distances),
            [jax.ShapeDtypeStruct((size, chans), BF if k else F32) for k in distances],
            [SM, VM, VM],
            [VM] * len(distances),
        )(ids, keep, got)

    if size % 16 == 0 and levels % 2 == 0:
        half = [jax.ShapeDtypeStruct((levels // 2, size, chans), BF)] * 2
        term = pltpu.VMEM((15 * chans, chans), BF)
        right, keep, send = call(
            functools.partial(half_kernel, dims, n, True, levels),
            [right_shape] + half,
            [SM, VM] + [VM] * n,
            [VM] * 3,
            [term],
            flops=n * unit_flops // 2,
        )(ids, turned, *grads_home[::-1])
        got = swap(send, "dp", 1)
        near_keep, near_send = call(
            functools.partial(half_kernel, dims, n, False, levels),
            half,
            [SM, VM, VM],
            [VM] * 2,
            [term],
            flops=n * unit_flops // 2,
        )(ids, turned, right)
        near_send, got = lax.optimization_barrier((near_send, got))
        near_got = swap(near_send, "dp", 1)
        far = range(levels // 2, levels)
        zsends = dict(zip(far, pair(keep, got, far)))
        near = range(levels // 2)
        zsends.update(zip(near, pair(near_keep, near_got, near)))
    else:
        term = call(
            functools.partial(term_kernel, dims, n),
            jax.ShapeDtypeStruct((27 * chans, chans), BF),
            [VM] * (1 + n),
            VM,
            [pltpu.VMEM(right_shape.shape, BF)],
            flops=n * unit_flops,
        )(turned, *grads_home)
        shares = term.reshape(levels, 2, size, chans)
        keep = lax.dynamic_index_in_dim(shares, core, 1, False)
        got = swap(lax.dynamic_index_in_dim(shares, 1 - core, 1, False), "dp", 1)
        zsends = dict(enumerate(pair(keep, got, range(levels))))
    own = zsends[0]
    arrived = [swap(zsends[k], "dp", 2 * k) for k in (*range(levels // 2, levels), *range(1, levels // 2))]

    late, own = lax.optimization_barrier((ids, own))
    (ing,) = home_backward(0, n, (), late)
    (seg,) = home_forward(n // 2, n, seg_early, late)

    scale = 1.0 / math.sqrt(micro * clips * ranks * points)
    share = call(
        functools.partial(sum_kernel, scale),
        jax.ShapeDtypeStruct((size, chans), F32),
        [VM] * levels,
        VM,
    )(own, *arrived)

    shape = (1, micro, clips, frames, rows, cols, chans)
    return (seg.reshape(shape), ing.reshape(shape), share.reshape(1, size * chans))


def solution(mesh):
    in_specs = (
        P(None, "dp", None, None, None, None),
        P(None, "dp", None, None, None, None),
        P("pipe", None, None),
        P("pipe", None),
    )
    out_specs = (
        P("pipe", None, "dp", None, None, None, None),
        P("pipe", None, "dp", None, None, None, None),
        P("pipe", "dp"),
    )
    return jax.shard_map(body, mesh=mesh, in_specs=in_specs, out_specs=out_specs, check_vma=False)
```

```python
import functools
import math

import jax
import jax.numpy as jnp
from jax import lax
from jax.experimental import pallas as pl
from jax.experimental.pallas import tpu as pltpu
from jax.sharding import PartitionSpec as P

GROUPS = 32
EPS = 1e-06
BF, F32 = jnp.bfloat16, jnp.float32
VMEM_LIMIT = 28 * 1024 * 1024
VM = pl.BlockSpec(memory_space=pltpu.VMEM)
SM = pl.BlockSpec(memory_space=pltpu.SMEM)
ANY = pl.BlockSpec(memory_space=pl.ANY)
HBM = pl.BlockSpec(memory_space=pltpu.HBM)


def call(kernel, out_shape, in_specs, out_specs, scratch=(), flops=0, moved=0, limit=VMEM_LIMIT):
    return pl.pallas_call(
        kernel,
        out_shape=out_shape,
        in_specs=in_specs,
        out_specs=out_specs,
        scratch_shapes=list(scratch),
        compiler_params=pltpu.CompilerParams(vmem_limit_bytes=limit),
        cost_estimate=pl.CostEstimate(flops=flops, bytes_accessed=moved, transcendentals=0),
    )


def swap(value, axis, bits):
    count = lax.axis_size(axis)
    return lax.ppermute(value, axis, [(i, i ^ bits) for i in range(count)])


def lane_partner(row, step):
    lane = lax.broadcasted_iota(jnp.int32, row.shape, 1)
    ahead = pltpu.roll(row, row.shape[1] - step, 1)
    return jnp.where((lane & step) == 0, ahead, pltpu.roll(row, step, 1))


def tree(parts):
    parts = list(parts)
    while len(parts) > 1:
        pairs = [u + v for u, v in zip(parts[::2], parts[1::2])]
        parts = pairs + parts[len(pairs) * 2 :]
    return parts[0]


def tiles(values):
    return [values[i : i + 8] for i in range(0, values.shape[0], 8)]


def group_sum(values, width):
    row = tree(tiles(values))
    for step in (4, 2, 1):
        row = row + pltpu.roll(row, step, 0)
    step = 1
    while step < width:
        row = row + lane_partner(row, step)
        step *= 2
    return row


def statistics(x32, width):
    parts = tiles(x32)
    pivot = parts[0]
    gaps = [part - pivot for part in parts[1:]]
    first = tree(gaps)
    second = tree([gap * gap for gap in gaps])
    count = float(len(parts))
    mean = pivot + first * (1.0 / count)
    spread = jnp.maximum(second - first * first * (1.0 / count), 0.0)

    def join(mean, spread, other, other_spread):
        gap = mean - other
        return (mean + other) * 0.5, spread + other_spread + gap * gap * (0.5 * count)

    for step in (4, 2, 1):
        mean, spread = join(mean, spread, pltpu.roll(mean, step, 0), pltpu.roll(spread, step, 0))
        count *= 2.0
    step = 1
    while step < width:
        mean, spread = join(mean, spread, lane_partner(mean, step), lane_partner(spread, step))
        count *= 2.0
        step *= 2
    return mean, lax.rsqrt(spread * (1.0 / count) + EPS)


def side(frame, cols, step):
    lines = frame.reshape(-1, cols, frame.shape[1])
    moved = pltpu.roll(lines, (-step) % cols, 1)
    col = lax.broadcasted_iota(jnp.int32, lines.shape, 1)
    keep = col < cols - 1 if step > 0 else col > 0
    return jnp.where(keep, moved, 0.0).reshape(frame.shape)


def row_shift(frame, cols, step):
    gap = jnp.zeros((cols, frame.shape[1]), frame.dtype)
    if step > 0:
        return jnp.concatenate([frame[cols:], gap], axis=0)
    return jnp.concatenate([gap, frame[:-cols]], axis=0)


def three_rows(frame, cols, steps):
    return [(frame if step == 0 else row_shift(frame, cols, step)).astype(BF) for step in steps]


def put_rows(spread, index, a, pieces):
    for b, piece in enumerate(pieces):
        chans = piece.shape[1]
        at = (3 * a + b) * chans
        spread[index, :, at : at + chans] = piece


def join_cols(parts, cols, chans, steps):
    total = None
    for at, step in enumerate(steps):
        piece = parts[:, at * chans : (at + 1) * chans]
        piece = piece if step == 0 else side(piece, cols, step)
        total = piece if total is None else total + piece
    return total


def copies_of(chunks, halves, target, sem):
    quarter = chunks[0].shape[1]
    return [
        pltpu.make_async_copy(
            ref.at[0 : target.shape[0]], target.at[:, pl.ds(pl.multiple_of(at * quarter, quarter), quarter), :], sem
        )
        for ref, at in zip(chunks, halves)
    ]


def piece_ids(ids, n_chunk):
    per = n_chunk // 2
    return [ids[1] * per + j for j in range(per)] + [(1 - ids[1]) * per + j for j in range(per)]


def forward_matrix(taps):
    chans = taps.shape[-1]
    parts = taps.reshape(9, 3, chans, chans)
    return jnp.concatenate([parts[:, c].reshape(9 * chans, chans) for c in range(3)], axis=1)


def backward_matrix(taps):
    chans = taps.shape[-1]
    parts = taps.reshape(9, 3 * chans, chans)
    return jnp.concatenate([parts[ab] for ab in range(9)], axis=1)


def norm_parts(x32, mean, rstd, gain):
    normed = (x32 - mean) * rstd
    scaled = normed * gain
    return normed, scaled, 0.5 * jnp.tanh(0.5 * scaled) + 0.5


def full(row, count):
    return jnp.broadcast_to(row[:1], (count, row.shape[1]))


def spread_forward(dims, values, found, gain, spread):
    frames, rows, cols, chans = dims
    plane, points = rows * cols, frames * rows * cols
    for k, x32 in enumerate(values):
        mean, rstd = found[k]
        _, scaled, gate = norm_parts(x32, full(mean, points), full(rstd, points), full(gain, points))
        act = scaled * gate
        for source in range(frames):
            pieces = three_rows(act[source * plane : (source + 1) * plane], cols, (-1, 0, 1))
            for f in range(frames):
                for a in range(3):
                    if max(f - 2 + a, 0) == source:
                        put_rows(spread, k * frames + f, a, pieces)


def forward_kernel(sections, dims, ids, x_ref, *refs):
    frames, rows, cols, chans = dims
    plane = rows * cols
    n_chunk = (len(refs) - 7 - sections) // sections
    chunks = [refs[k * n_chunk : (k + 1) * n_chunk] for k in range(sections)]
    refs = refs[sections * n_chunk :]
    outs, stats, every = refs[:3]
    sends = refs[3 : 3 + sections]
    spread, product, inputs, sems = refs[3 + sections :]
    place = ids[0]
    taps = every.shape[1]
    for k in range(sections):
        for copy in copies_of(chunks[k], piece_ids(ids, n_chunk), every.at[k], sems.at[k]):
            copy.start()
    for k in range(sections):
        parts = chunks[k][0][taps].astype(F32)
        stats[place ^ k, 16:24] = full(parts[0:1] + parts[1:2] + parts[2:3], 8)
    x = x_ref[...]
    for unit in range(sections):
        inputs[unit] = x
        x32 = x.astype(F32)
        mean, rstd = statistics(x32, chans // GROUPS)
        stats[unit, 0:8], stats[unit, 8:16] = mean, rstd
        spread_forward(dims, [x32], [(mean, rstd)], stats[unit, 16:17], spread)
        source = place ^ unit
        pltpu.make_async_copy(every.at[source], every.at[source], sems.at[source]).wait()
        lhs = spread[...].reshape(frames * plane, 9 * chans)
        product[...] = jnp.dot(lhs, forward_matrix(every[source]), preferred_element_type=F32)
        for f in range(frames):
            spot = slice(f * plane, (f + 1) * plane)
            joined = join_cols(product[spot], cols, chans, (-1, 0, 1))
            outs[unit, spot] = (x32[spot] + joined).astype(BF)
        x = outs[unit]
    for k in range(sections):
        sends[k][...] = inputs[place ^ k]


def turn_kernel(dims, n, ids, unit_stats, *refs):
    frames, rows, cols, chans = dims
    plane, points = rows * cols, frames * rows * cols
    xs, (turned, stats) = refs[:n], refs[n:]
    gain = unit_stats[ids[0], 16:24]
    for k in range(n):
        x32 = xs[k][...].astype(F32)
        mean, rstd = statistics(x32, chans // GROUPS)
        stats[k, 0:8], stats[k, 8:16], stats[k, 16:24] = mean, rstd, gain
        _, scaled, gate = norm_parts(x32, full(mean, points), full(rstd, points), full(gain, points))
        act = (scaled * gate).astype(BF).astype(F32)
        for f in range(frames):
            frame = act[f * plane : (f + 1) * plane]
            for at, step in enumerate((-1, 0, 1)):
                piece = frame if step == 0 else side(frame, cols, step)
                turned[at * chans : (at + 1) * chans, pl.ds((f * n + k) * plane, plane)] = piece.T.astype(BF)


def home_forward_kernel(dims, n, first, last, ids, stats, own, *refs):
    frames, rows, cols, chans = dims
    plane = rows * cols
    count = last - first
    xs, refs = refs[:count], refs[count:]
    done = refs[:first] if last == n else ()
    outs, spread = refs[len(done) : -1], refs[-1]
    for k in range(len(done)):
        outs[0][lax.rem(ids[0] ^ k, n)] = done[k][...]
    values = [ref[...].astype(F32) for ref in xs]
    known = [(stats[first + i, 0:8], stats[first + i, 8:16]) for i in range(count)]
    spread_forward(dims, values, known, stats[0, 16:17], spread)
    lhs = spread[...].reshape(count * frames * plane, 9 * chans)
    product = jnp.dot(lhs, forward_matrix(own[...]), preferred_element_type=F32)
    for i in range(count):
        at = lax.rem(ids[0] ^ (first + i), n)
        for f in range(frames):
            spot = slice(f * plane, (f + 1) * plane)
            joined = join_cols(product[(i * frames + f) * plane : (i * frames + f + 1) * plane], cols, chans, (-1, 0, 1))
            result = (values[i][spot] + joined).astype(BF)
            if last == n:
                outs[0][at, spot] = result
            else:
                outs[i][spot] = result


def unit_backward(dims, x32, grad, stat, gain, multiply, spread):
    frames, rows, cols, chans = dims
    plane, points = rows * cols, frames * rows * cols
    width = chans // GROUPS
    count = float(points * width)
    g32 = grad.astype(F32)
    per = [g32[f * plane : (f + 1) * plane] for f in range(frames)]
    for f in range(frames):
        for a in range(3):
            sources = [q for q in range(frames) if max(q - 2 + a, 0) == f]
            if sources:
                total = functools.reduce(lambda u, v: u + v, [per[q] for q in sources])
                put_rows(spread, f, a, three_rows(total, cols, (1, 0, -1)))
            else:
                put_rows(spread, f, a, [jnp.zeros((plane, chans), BF)] * 3)
    product = multiply(spread[...].reshape(points, 9 * chans))
    gact = jnp.concatenate(
        [join_cols(product[f * plane : (f + 1) * plane], cols, chans, (1, 0, -1)) for f in range(frames)], axis=0
    )
    rstd = full(stat[8:16], points)
    wide_gain = full(gain, points)
    normed, scaled, gate = norm_parts(x32, full(stat[0:8], points), rstd, wide_gain)
    d_normed = gact * (gate * (1.0 + scaled * (1.0 - gate))) * wide_gain
    m1 = group_sum(d_normed, width) * (1.0 / count)
    m2 = group_sum(d_normed * normed, width) * (1.0 / count)
    dx = rstd * (d_normed - full(m1, points) - normed * full(m2, points))
    return (g32 + dx).astype(BF)


def times_transposed(lhs, taps):
    return lax.dot_general(lhs, backward_matrix(taps), (((1,), (1,)), ((), ())), preferred_element_type=F32)


def backward_kernel(sections, dims, ids, outs, grad_ref, stats, every, *refs):
    sends, (spread, grads) = refs[:sections], refs[sections:]
    place = ids[0]
    grad = grad_ref[...]
    grads[sections - 1] = grad
    for unit in range(sections - 1, 0, -1):

        def multiply(lhs, unit=unit):
            return times_transposed(lhs, every[place ^ unit])

        grad = unit_backward(dims, outs[unit - 1].astype(F32), grad, stats[unit], stats[unit, 16:17], multiply, spread)
        grads[unit - 1] = grad
    for k in range(sections):
        sends[k][...] = grads[place ^ k]


def home_backward_kernel(dims, n, first, last, ids, stats, own, *refs):
    count = last - first
    xs, grads = refs[:count], refs[count : 2 * count]
    refs = refs[2 * count :]
    done = refs[:first] if last == n else ()
    outs, spread = refs[len(done) : -1], refs[-1]
    place = ids[0]
    for k in range(len(done)):
        outs[0][(place ^ k) % n] = done[k][...]
    for i in range(count):
        result = unit_backward(
            dims,
            xs[i][...].astype(F32),
            grads[i][...],
            stats[first + i],
            stats[0, 16:17],
            lambda lhs: times_transposed(lhs, own[...]),
            spread,
        )
        if last == n:
            outs[0][(place ^ (first + i)) % n] = result
        else:
            outs[i][...] = result


def tap_spots(frames, n, plane):
    spots = [0]
    for a in range(3):
        spots.append(spots[-1] + max(1, frames - 2 + a) * n * plane)
    return spots


def put_right(dims, n, grads, right):
    frames, rows, cols, chans = dims
    plane = rows * cols
    spots = tap_spots(frames, n, plane)
    for k in range(n):
        mine = grads[k][...].astype(F32)
        per = [mine[f * plane : (f + 1) * plane] for f in range(frames)]
        for a in range(3):
            folded = [f for f in range(frames) if f - 2 + a <= 0]
            groups = [folded] + [[f] for f in range(frames) if f - 2 + a > 0]
            for i, group in enumerate(groups):
                total = functools.reduce(lambda u, v: u + v, [per[f] for f in group])
                at = spots[a] + (i * n + k) * plane
                for b, piece in enumerate(three_rows(total, cols, (1, 0, -1))):
                    right[at : at + plane, b * chans : (b + 1) * chans] = piece


def put_term(dims, n, a, taps, turned, right, term, base):
    frames, rows, cols, chans = dims
    spots = tap_spots(frames, n, rows * cols)
    used = spots[a + 1] - spots[a]
    rhs = right[spots[a] : spots[a + 1], taps[0] * chans : (taps[-1] + 1) * chans]
    out = jnp.dot(turned[:, 0:used], rhs, preferred_element_type=F32)
    for b in range(len(taps)):
        for c in range(3):
            block = out[c * chans : (c + 1) * chans, b * chans : (b + 1) * chans]
            term[pl.ds(base + (b * 3 + c) * chans, chans), :] = block.astype(BF)


def term_kernel(dims, n, turned, *refs):
    grads, (term, right) = refs[:n], refs[n:]
    put_right(dims, n, grads, right)
    for a in range(3):
        put_term(dims, n, a, (0, 1, 2), turned, right, term, a * 9 * dims[3])


def half_kernel(dims, n, far, levels, ids, turned, *refs):
    chans = dims[3]
    if far:
        put_right(dims, n, refs[:n][::-1], refs[n])
        refs = refs[n:]
    right, keep, send, term = refs
    upper = ids[2] >= levels // 2

    def low():
        put_term(dims, n, 0, (0, 1, 2), turned, right, term, 0)
        put_term(dims, n, 1, (0, 1), turned, right, term, 9 * chans)

    def high():
        put_term(dims, n, 1, (1, 2), turned, right, term, 0)
        put_term(dims, n, 2, (0, 1, 2), turned, right, term, 6 * chans)

    wants_high = jnp.logical_not(upper) if far else upper
    pl.when(wants_high)(high)
    pl.when(jnp.logical_not(wants_high))(low)
    skip = jnp.where(wants_high, 27 * chans // 2 - 12 * chans, 0)
    core = ids[1]
    size = keep.shape[1]
    for j in range(levels // 2):
        here = pl.multiple_of(skip + (2 * j + core) * size, 16)
        there = pl.multiple_of(skip + (2 * j + 1 - core) * size, 16)
        keep[j] = term[pl.ds(here, size), :]
        send[j] = term[pl.ds(there, size), :]


def pair_kernel(distances, ids, keep, got, *sends):
    for k, out in zip(distances, sends):
        at = lax.rem(ids[2] ^ k, keep.shape[0])
        out[...] = (keep[at].astype(F32) + got[at].astype(F32)).astype(out.dtype)


def sum_kernel(scale, own, *refs):
    total = own[...]
    for ref in refs[:-1]:
        total = total + ref[...].astype(F32)
    refs[-1][...] = total * scale


def with_gains(piece, gains):
    taps, rows, chans = piece.shape
    high = lax.reduce_precision(gains, 8, 7)
    middle = lax.reduce_precision(gains - high, 8, 7)
    low = gains - high - middle
    shape = (taps + 1, rows, chans)
    row = lax.broadcasted_iota(jnp.int32, shape, 1)
    extra = jnp.where(row == 0, high[None], jnp.where(row == 1, middle[None], low[None])).astype(BF)
    padded = lax.pad(piece, jnp.zeros((), BF), ((0, 1, 0), (0, 0, 0), (0, 0, 0)))
    return jnp.where(lax.broadcasted_iota(jnp.int32, shape, 0) < taps, padded, extra)


def gather_chunks(mine, sections, ride):
    parts = len(mine)
    got = {}
    if sections == 4 and parts == 2:
        first = swap(mine[0], "pipe", 1)
        second = swap(mine[1], "pipe", 2)
        first, *ride = lax.optimization_barrier((first, *ride))
        got[1] = [first, swap(mine[1], "pipe", 1)]
        got[2] = [swap(mine[0], "pipe", 2), second]
        got[3] = [swap(first, "pipe", 2), swap(second, "pipe", 1)]
    else:
        for k in range(1, sections):
            got[k] = [swap(piece, "pipe", k) for piece in mine]
    return got, ride


def body(video, cotangent, weights, gains):
    sections = lax.axis_size("pipe")
    ranks = lax.axis_size("dp")
    place = lax.axis_index("pipe")
    rank = lax.axis_index("dp")
    core = lax.rem(rank, 2)
    micro, clips, frames, rows, cols, chans = video.shape
    ids = jnp.stack([place, core, lax.div(rank, 2)]).astype(jnp.int32)
    points = frames * rows * cols
    dims = (frames, rows, cols, chans)
    parts = 2
    n_chunk = 2 * parts
    quarter = chans // n_chunk

    video = video.reshape(micro, points, chans)
    cot = cotangent.reshape(micro, points, chans)
    kernel_rows = weights.reshape(27, chans, chans)
    cut = kernel_rows.reshape(27, n_chunk, quarter, chans)
    mine = [lax.dynamic_index_in_dim(cut, core * parts + j, 1, False) for j in range(parts)]
    mine[0] = with_gains(mine[0], gains)
    x = lax.dynamic_index_in_dim(video, lax.rem(place, micro), 0, False)
    grad = lax.dynamic_index_in_dim(cot, lax.rem(place, micro), 0, False)
    got, (x, grad) = gather_chunks(mine, sections, (x, grad))
    got[0] = list(mine)
    flat = [piece for k in range(sections) for piece in got[k] + [swap(piece, "dp", 1) for piece in got[k]]]

    act_shape = jax.ShapeDtypeStruct((points, chans), BF)
    unit_flops = 2 * points * 27 * chans * chans
    n = min(sections, micro)
    spots = sum(max(1, frames - 2 + a) for a in range(3))

    def spread(count):
        return pltpu.VMEM((count * frames, rows * cols, 9 * chans), BF)

    product = pltpu.VMEM((points, 3 * chans), F32)

    outs, stats, every, *xsends = call(
        functools.partial(forward_kernel, sections, dims),
        [
            jax.ShapeDtypeStruct((sections, points, chans), BF),
            jax.ShapeDtypeStruct((sections, 24, chans), F32),
            jax.ShapeDtypeStruct((sections, 27, chans, chans), BF),
        ]
        + [act_shape] * sections,
        [SM, VM] + [ANY if i % n_chunk else VM for i in range(len(flat))],
        [VM] * (3 + sections),
        [
            spread(1),
            product,
            pltpu.VMEM((sections, points, chans), BF),
            pltpu.SemaphoreType.DMA((sections,)),
        ],
        flops=4 * sections * unit_flops,
    )(ids, x, *flat)
    xs_home = [xsends[0]] + [swap(xsends[k], "pipe", k) for k in range(1, n)]

    gsends = call(
        functools.partial(backward_kernel, sections, dims),
        [act_shape] * sections,
        [SM] + [VM] * 4,
        [VM] * sections,
        [spread(1), pltpu.VMEM((sections, points, chans), BF)],
        flops=4 * (sections - 1) * unit_flops,
    )(ids, outs, grad, stats, every)
    grads_home = [gsends[0]] + [swap(gsends[k], "pipe", k) for k in range(1, n)]

    turned, home_stats = call(
        functools.partial(turn_kernel, dims, n),
        [jax.ShapeDtypeStruct((3 * chans, n * points), BF), jax.ShapeDtypeStruct((n, 24, chans), F32)],
        [SM] + [VM] * (1 + n),
        [VM] * 2,
        flops=n * unit_flops,
    )(ids, stats, *xs_home)

    def home_forward(first, last, done, ids):
        count = last - first
        return call(
            functools.partial(home_forward_kernel, dims, n, first, last),
            [jax.ShapeDtypeStruct((micro, points, chans), BF)] if last == n else [act_shape] * count,
            [SM, VM, VM] + [VM] * (count + len(done)),
            [VM] * (1 if last == n else count),
            [spread(count)],
            flops=4 * count * unit_flops,
        )(ids, home_stats, kernel_rows, *xs_home[first:last], *done)

    def home_backward(first, last, done, ids):
        count = last - first
        return call(
            functools.partial(home_backward_kernel, dims, n, first, last),
            [jax.ShapeDtypeStruct((micro, points, chans), BF)] if last == n else [act_shape] * count,
            [SM, VM, VM] + [VM] * (2 * count + len(done)),
            [VM] * (1 if last == n else count),
            [spread(1)],
            flops=4 * count * unit_flops,
        )(ids, home_stats, kernel_rows, *xs_home[first:last], *grads_home[first:last], *done)

    seg_early = home_forward(0, n // 2, (), ids)
    turned, *seg_early = lax.optimization_barrier((turned, *seg_early))

    size = 27 * chans // ranks
    levels = ranks // 2
    right_shape = jax.ShapeDtypeStruct((tap_spots(frames, n, rows * cols)[-1], 3 * chans), BF)

    def pair(keep, got, distances):
        return call(
            functools.partial(pair_kernel, distances),
            [jax.ShapeDtypeStruct((size, chans), BF if k else F32) for k in distances],
            [SM, VM, VM],
            [VM] * len(distances),
        )(ids, keep, got)

    if size % 16 == 0 and levels % 2 == 0:
        half = [jax.ShapeDtypeStruct((levels // 2, size, chans), BF)] * 2
        term = pltpu.VMEM((15 * chans, chans), BF)
        right, keep, send = call(
            functools.partial(half_kernel, dims, n, True, levels),
            [right_shape] + half,
            [SM, VM] + [VM] * n,
            [VM] * 3,
            [term],
            flops=n * unit_flops // 2,
        )(ids, turned, *grads_home[::-1])
        got = swap(send, "dp", 1)
        near_keep, near_send = call(
            functools.partial(half_kernel, dims, n, False, levels),
            half,
            [SM, VM, VM],
            [VM] * 2,
            [term],
            flops=n * unit_flops // 2,
        )(ids, turned, right)
        near_send, got = lax.optimization_barrier((near_send, got))
        near_got = swap(near_send, "dp", 1)
        far = range(levels // 2, levels)
        zsends = dict(zip(far, pair(keep, got, far)))
        near = range(levels // 2)
        zsends.update(zip(near, pair(near_keep, near_got, near)))
    else:
        term = call(
            functools.partial(term_kernel, dims, n),
            jax.ShapeDtypeStruct((27 * chans, chans), BF),
            [VM] * (1 + n),
            VM,
            [pltpu.VMEM(right_shape.shape, BF)],
            flops=n * unit_flops,
        )(turned, *grads_home)
        shares = term.reshape(levels, 2, size, chans)
        keep = lax.dynamic_index_in_dim(shares, core, 1, False)
        got = swap(lax.dynamic_index_in_dim(shares, 1 - core, 1, False), "dp", 1)
        zsends = dict(enumerate(pair(keep, got, range(levels))))
    own = zsends[0]
    arrived = [swap(zsends[k], "dp", 2 * k) for k in (*range(levels // 2, levels), *range(1, levels // 2))]

    late, own = lax.optimization_barrier((ids, own))
    (ing,) = home_backward(0, n, (), late)
    (seg,) = home_forward(n // 2, n, seg_early, late)

    scale = 1.0 / math.sqrt(micro * clips * ranks * points)
    share = call(
        functools.partial(sum_kernel, scale),
        jax.ShapeDtypeStruct((size, chans), F32),
        [VM] * levels,
        VM,
    )(own, *arrived)

    shape = (1, micro, clips, frames, rows, cols, chans)
    return (seg.reshape(shape), ing.reshape(shape), share.reshape(1, size * chans))


def solution(mesh):
    in_specs = (
        P(None, "dp", None, None, None, None),
        P(None, "dp", None, None, None, None),
        P("pipe", None, None),
        P("pipe", None),
    )
    out_specs = (
        P("pipe", None, "dp", None, None, None, None),
        P("pipe", None, "dp", None, None, None, None),
        P("pipe", "dp"),
    )
    return jax.shard_map(body, mesh=mesh, in_specs=in_specs, out_specs=out_specs, check_vma=False)
```
